256 devices in a mesh: grp: 8 (over y, core), ctx: 32 (over x, z).
Axes of the slice: x: 4, y: 4, z: 8, core: 2. Of those that a mesh axis runs over, the one named last changes fastest.
Arguments:
- queries: bfloat16 [128, 8192], P('grp'), may hold values from -250 to 250
- resident_key_cache: bfloat16 [128, 4096, 512], P('grp', 'ctx'), may hold values from -6 to 6
- resident_value_cache: bfloat16 [128, 4096, 512], P('grp', 'ctx'), may hold values from -6 to 6
- res_len: int32 [128], P('grp'), may hold values from 2 to 4096, as said below
- visual_page_pool: bfloat16 [4096, 2, 8, 512], P(('grp', 'ctx')), may hold values from -6 to 6
- recall_holder: int32 [32, 128, 16], P('ctx', 'grp'), may hold values from 0 to 255, all different within a row; in each aligned block of 16 rows (0 to 15, 16 to 31, ..., all dimensions but the last counted through in order) at most 2 rows name the same one
- recall_slot: int32 [32, 128, 16], P('ctx', 'grp'), may hold values from 0 to 15
- o_weight: bfloat16 [8192, 4096], P('ctx'), may hold values from -3 to 3
- residual: bfloat16 [128, 4096], P('grp'), may hold values from -60 to 60
- norm_gain: float32 [4096], replicated, may hold values from 0.5 to 1.5
- expert_ids: int32 [128, 8], P('grp'), may hold values from 0 to 63, all different within a row; in each aligned block of 16 rows (0 to 15, 16 to 31, ...) at most 4 rows name the same one
- expert_weights: float32 [128, 8], P('grp'), may hold values from 1 to 4
- w_gate: bfloat16 [256, 192, 4096], P(('grp', 'ctx')), may hold values from -0.09375 to 0.09375
- w_up: bfloat16 [256, 192, 4096], P(('grp', 'ctx')), may hold values from -0.09375 to 0.09375
- w_down: bfloat16 [256, 192, 4096], P(('grp', 'ctx')), may hold values from -0.21875 to 0.21875
Outputs:
- mixed: bfloat16 [128, 4096], P('grp', 'ctx')
The draws below stay inside these ranges and needn't reach their ends.
Inputs may be any that keep to these rules, and one draw needn't show every extreme that they name: `res_len`: some request has length 4096 and some has length 2. `recall_holder`: the 16 holders of one request on one index of ctx differ; among the rows of one device (one index of ctx, the 16 requests of one group) no holder is named by more than 2 requests, and in some device's rows one holder by exactly 2. `expert_ids`: the 8 experts of a token differ; among the 16 tokens of one group no expert is named more than 4 times, and in some group one expert exactly 4 times.
All inputs are finite; a program needn't handle non-finite values.
Results may differ from the reference program's by a relative error of at most 0.025.
Values may be sent and summed in bfloat16 or wider, within the bound.
No kernel may reach another device: no remote copies, remote signals or barrier semaphores. Data moves between devices by JAX's collectives and lax.ppermute only.
A program may use at most 128 MiB of HBM per device.

```python
import math
import jax
import jax.numpy as jnp
import numpy as np
from jax import lax

D = 4096
QUERY_HEADS = 64
KEY_VALUE_HEADS = 4
HEAD_WIDTH = 128
EFF = 768
TOPK = 8
CAPE = 4
PAGE_TOKENS = 8
PG_DEV = 16
REQ = 16
EXPERTS = 64
PARTS_SIZE = 4
EPART = 192
REQUEST_COUNT = 128
CONTEXT_LENGTH = 4096
CAP = 2
PAGES_PER_UNIT = 16
N_CTX = 32
DEVICES = 256


def draw_queries(key, part):
    start_offset = jax.random.truncated_normal(jax.random.fold_in(key, 6), -6.0, 6.0, (REQUEST_COUNT, KEY_VALUE_HEADS, QUERY_HEADS // KEY_VALUE_HEADS, HEAD_WIDTH), jnp.float32)
    return start_offset.reshape(REQUEST_COUNT, QUERY_HEADS * HEAD_WIDTH).astype(jnp.bfloat16)


def draw_resident_key_cache(key, part):
    random_noise = jax.random.truncated_normal(jax.random.fold_in(key, 5), -6.0, 6.0, (REQUEST_COUNT, CONTEXT_LENGTH, KEY_VALUE_HEADS * HEAD_WIDTH), jnp.float32)
    return random_noise.astype(jnp.bfloat16)


def draw_residual(key, part):
    start_offset = jax.random.truncated_normal(jax.random.fold_in(key, 31), -4.0, 4.0, (REQUEST_COUNT, D), jnp.float32)
    return start_offset.astype(jnp.bfloat16)


def draw_res_len(key, part):
    lengths = jax.random.randint(jax.random.fold_in(key, 21), (REQUEST_COUNT,), 2, CONTEXT_LENGTH + 1)
    chosen = jax.random.randint(jax.random.fold_in(key, 22), (), 0, REQUEST_COUNT)
    lengths = lengths.at[chosen].set(CONTEXT_LENGTH)
    lengths = lengths.at[(chosen + REQUEST_COUNT // 2) % REQUEST_COUNT].set(2)
    return lengths.astype(jnp.int32)


def set_ends(array, key, smallest, high):
    longest = array.shape.index(max(array.shape))
    spots = []
    for shift in (0, 1):
        where = [jax.random.randint(jax.random.fold_in(key, axis), (), 0, length) for axis, length in enumerate(array.shape)]
        where[longest] = (where[longest] + shift) % array.shape[longest]
        spots.append(tuple(where))
    return array.at[spots[0]].set(smallest).at[spots[1]].set(high)


def shard_levels(rng, shape, pieces, smallest, largest):
    def one(dim, shards_of):
        steps = jax.random.uniform(jax.random.fold_in(jax.random.fold_in(rng, 6), dim), (shards_of,), jnp.float32, smallest / len(pieces), largest / len(pieces))
        return jnp.repeat(jnp.exp(steps), shape[dim] // shards_of).reshape((-1,) + (1,) * (len(shape) - dim - 1))

    level = one(*pieces[0])
    for cut in pieces[1:]:
        level = level * one(*cut)
    return level


def assign_block(own_key, own, number, rows, count, top, reach, slope):
    ranking = jax.random.permutation(own_key, count)
    heavy_load, common = load_shares(count, rows * top, reach, slope, True), load_shares(count, rows * top, reach, slope, False)
    places = jnp.arange(count)

    def named(sizes, rotation):
        used = int((sizes > 0).sum())
        fixed = max(1, used // 4)
        shifted = fixed + (places - fixed + rotation * (used - fixed)) % max(1, count - fixed)
        return jnp.zeros((count,), jnp.int32).at[ranking[jnp.where(places < fixed, places, shifted)]].set(jnp.asarray(sizes, jnp.int32))

    sizes = jnp.where(number % 4 == 0, named(heavy_load, number // 4), named(common, number - number // 4 - 1))
    mixed = jax.random.permutation(jax.random.fold_in(own, 3), count)
    donor, taker = mixed[0:count // 2 * 2:2], mixed[1:count // 2 * 2:2]
    margin = jnp.minimum(sizes[donor] - 1, reach - sizes[taker]) // 2
    margin = jnp.where((donor == ranking[0]) | (taker == ranking[0]) | (sizes[taker] == 0), 0, jnp.maximum(margin, 0))
    shifted = jax.random.randint(jax.random.fold_in(own, 4), (count // 2,), 0, 1 << 20) % (margin + 1)
    sizes = sizes.at[donor].add(-shifted).at[taker].add(shifted)
    labels = jnp.searchsorted(jnp.cumsum(sizes), jnp.arange(rows * top), side="right").astype(jnp.int32)
    table = labels.reshape(top, rows).T
    table = table[jax.random.permutation(jax.random.fold_in(own, 1), rows)]
    rotation = jax.random.randint(jax.random.fold_in(own, 2), (rows, 1), 0, top)
    return jnp.take_along_axis(table, (jnp.arange(top)[None, :] + rotation) % top, axis=1)


def load_shares(count, total, reach, lean, full):
    portions = [(1 << 20) // math.isqrt(grade ** lean) + 1 for grade in range(1, count + 1)]
    largest = reach if full else min(reach, max(-(-total // count), total * portions[0] // sum(portions)))
    least = 1 if total - largest >= count - 1 else 0
    counts, surplus = [largest] + [least] * (count - 1), total - largest - least * (count - 1)
    while surplus > 0:
        movable = [i for i in range(1, count) if counts[i] < largest] or [i for i in range(1, count) if counts[i] < reach]
        mass, left = sum([portions[i] for i in movable]), surplus
        for i in movable:
            more = min(reach - counts[i], max(1, left * portions[i] // mass), surplus)
            counts[i] = counts[i] + more
            surplus = surplus - more
    return np.array(counts)


def centred(key, extent, deviation, limit, cuts=(), kind=jnp.bfloat16):
    entries = jax.random.normal(key, extent, jnp.float32) * deviation
    if len(cuts) > 0:
        entries = shard_levels(key, extent, cuts, -0.22, 0.18) * entries
    return jnp.clip(entries, min=-limit, max=limit).astype(kind)


def setup_inputs(seed: int = 0) -> dict:
    splits = jax.random.split(jax.random.key(seed), 16)
    queries = draw_queries(jax.random.fold_in(splits[15], 71), 0)
    resident_key_cache = draw_resident_key_cache(jax.random.fold_in(splits[15], 71), 0)
    resident_value_cache = centred(splits[2], (REQUEST_COUNT, CONTEXT_LENGTH, KEY_VALUE_HEADS * HEAD_WIDTH), 1.0, 6.0, ((0, 8), (1, 32)))
    res_len = draw_res_len(jax.random.fold_in(splits[15], 71), 0)
    visual_page_pool = centred(splits[4], (DEVICES * PAGES_PER_UNIT, 2, PAGE_TOKENS, KEY_VALUE_HEADS * HEAD_WIDTH), 1.0, 6.0, ((0, 256),))
    recall_holder_keys = jax.random.split(jax.random.fold_in(splits[5], 1), N_CTX * REQUEST_COUNT // REQ)
    recall_holder_turns = jax.random.permutation(jax.random.fold_in(splits[5], 3), N_CTX * REQUEST_COUNT // REQ)
    recall_holder = jax.vmap(lambda own, number: assign_block(jax.random.fold_in(splits[5], 2), own, number, REQ, DEVICES, PG_DEV, CAP, 2))(recall_holder_keys, recall_holder_turns).reshape((N_CTX, REQUEST_COUNT, PG_DEV))
    recall_slot = set_ends(jax.random.randint(splits[6], (N_CTX, REQUEST_COUNT, PG_DEV), 0, PAGES_PER_UNIT), jax.random.fold_in(splits[6], 1), 0, PAGES_PER_UNIT - 1).astype(jnp.int32)
    o_weight = centred(splits[7], (QUERY_HEADS * HEAD_WIDTH, D), 0.5, 3.0, ((0, 32),))
    residual = draw_residual(jax.random.fold_in(splits[15], 71), 0)
    norm_gain = jnp.clip(jax.random.uniform(splits[9], (D,), jnp.float32, 0.5, 1.5), 0.5, 1.5)
    expert_ids_keys = jax.random.split(jax.random.fold_in(splits[10], 1), REQUEST_COUNT // REQ)
    expert_ids_turns = jax.random.permutation(jax.random.fold_in(splits[10], 3), REQUEST_COUNT // REQ)
    expert_ids = jax.vmap(lambda own, number: assign_block(jax.random.fold_in(splits[10], 2), own, number, REQ, EXPERTS, TOPK, CAPE, 1))(expert_ids_keys, expert_ids_turns).reshape((REQUEST_COUNT, TOPK))
    expert_weights = jnp.clip(jnp.exp(math.log(4.0) - 1.3862944 * jax.random.uniform(splits[11], (REQUEST_COUNT, TOPK), jnp.float32) ** shard_levels(splits[11], (REQUEST_COUNT, TOPK), ((0, 8),), -0.2, 0.2)), 1.0, 4.0)
    w_gate = centred(splits[12], (EXPERTS * PARTS_SIZE, EPART, D), D ** -0.5, 0.09375, ((0, 256),))
    w_up = centred(splits[13], (EXPERTS * PARTS_SIZE, EPART, D), D ** -0.5, 0.09375, ((0, 256),))
    w_down = centred(splits[14], (EXPERTS * PARTS_SIZE, EPART, D), EFF ** -0.5, 0.21875, ((0, 256),))
    return dict(queries=queries, resident_key_cache=resident_key_cache, resident_value_cache=resident_value_cache, res_len=res_len, visual_page_pool=visual_page_pool, recall_holder=recall_holder, recall_slot=recall_slot, o_weight=o_weight, residual=residual, norm_gain=norm_gain, expert_ids=expert_ids, expert_weights=expert_weights, w_gate=w_gate, w_up=w_up, w_down=w_down)


VERY_NEGATIVE = -1e+30

def reference(queries, resident_key_cache, resident_value_cache, res_len, visual_page_pool, recall_holder, recall_slot, o_weight, residual, norm_gain, expert_ids, expert_weights, w_gate, w_up, w_down):
    head_groups = QUERY_HEADS // KEY_VALUE_HEADS
    score_scale = HEAD_WIDTH ** (-0.5)
    positions = jnp.arange(CONTEXT_LENGTH, dtype=jnp.int32)
    recall_count = N_CTX * PG_DEV * PAGE_TOKENS

    def attend(token_position):
        query_matrix = queries[token_position].reshape(KEY_VALUE_HEADS, head_groups, HEAD_WIDTH).astype(jnp.float32)
        page_ids = (recall_holder[:, token_position, :] * PAGES_PER_UNIT + recall_slot[:, token_position, :]).reshape(-1).astype(jnp.int32)
        page_row_list = jnp.take(visual_page_pool, page_ids, axis=0)
        joined_keys = jnp.concatenate([resident_key_cache[token_position], page_row_list[:, 0].reshape(recall_count, KEY_VALUE_HEADS * HEAD_WIDTH)], axis=0)
        joined_values = jnp.concatenate([resident_value_cache[token_position], page_row_list[:, 1].reshape(recall_count, KEY_VALUE_HEADS * HEAD_WIDTH)], axis=0)
        is_valid = jnp.concatenate([positions < res_len[token_position], jnp.ones((recall_count,), dtype=bool)])
        expanded_keys = joined_keys.reshape(-1, KEY_VALUE_HEADS, HEAD_WIDTH).astype(jnp.float32)
        expanded_values = joined_values.reshape(-1, KEY_VALUE_HEADS, HEAD_WIDTH).astype(jnp.float32)
        scores = jnp.einsum('kgd,nkd->kgn', query_matrix, expanded_keys) * score_scale
        scores = jnp.where(is_valid[None, None, :], scores, VERY_NEGATIVE)
        weights = jnp.exp(scores - lax.optimization_barrier(jnp.max(scores, axis=-1, keepdims=True)))
        weights = jnp.where(is_valid[None, None, :], weights, 0.0)
        row_total = lax.optimization_barrier(jnp.sum(weights, axis=-1))
        rounded = lax.optimization_barrier(weights.astype(jnp.bfloat16)).astype(jnp.float32)
        weighted_sum = jnp.einsum('kgn,nkd->kgd', rounded, expanded_values)
        return (weighted_sum / row_total[..., None]).astype(jnp.bfloat16).reshape(QUERY_HEADS * HEAD_WIDTH)
    attention = lax.map(attend, jnp.arange(REQUEST_COUNT, dtype=jnp.int32))
    projected = jnp.dot(attention, o_weight, preferred_element_type=jnp.float32)
    hidden = residual.astype(jnp.float32) + projected
    normed = (hidden * lax.rsqrt(lax.optimization_barrier(jnp.mean(hidden * hidden, axis=-1, keepdims=True)) + 1e-06) * norm_gain).astype(jnp.bfloat16)
    pair_token = jnp.arange(REQUEST_COUNT * TOPK, dtype=jnp.int32) // TOPK
    pair_expert = expert_ids.reshape(-1).astype(jnp.int32)
    part_rows = PARTS_SIZE * EPART

    def run_pair(pair_items):
        token_position, expert = pair_items
        first_row = (expert * PARTS_SIZE).astype(jnp.int32)
        gate_rows = lax.dynamic_slice_in_dim(w_gate, first_row, PARTS_SIZE, 0).reshape(part_rows, D)
        up_rows = lax.dynamic_slice_in_dim(w_up, first_row, PARTS_SIZE, 0).reshape(part_rows, D)
        down_rows = lax.dynamic_slice_in_dim(w_down, first_row, PARTS_SIZE, 0).reshape(part_rows, D)
        vector = normed[token_position]
        gate_value = jnp.dot(gate_rows, vector, preferred_element_type=jnp.float32)
        upward = jnp.dot(up_rows, vector, preferred_element_type=jnp.float32)
        activation = (jax.nn.silu(gate_value) * upward).astype(jnp.bfloat16)
        return jnp.dot(activation, down_rows, preferred_element_type=jnp.float32)
    outputs = lax.map(run_pair, (pair_token, pair_expert))
    mixture = lax.optimization_barrier(jnp.sum(outputs.reshape(REQUEST_COUNT, TOPK, D) * expert_weights[..., None], axis=1))
    return (hidden + mixture).astype(jnp.bfloat16)
```

```python
import jax
import jax.numpy as jnp
from jax import lax
from jax.experimental import pallas as pl
from jax.experimental.pallas import tpu as pltpu
from jax.sharding import Mesh, PartitionSpec as P

HEADS = 64
KV = 4
HPK = HEADS // KV
HW = 128
T = 16
D = 4096
NC = 32
NG = 8
CAPE = 4
FP = 192
TOK = 8
SLOTS = 16
EPS = 1e-06
NEG = -(2.0**100)
SCALE = HW**-0.5
BF = jnp.bfloat16
F32 = jnp.float32
GRP = ("y", "core")
CTX = ("x", "z")
ALL = GRP + CTX
NT = (((1,), (1,)), ((), ()))
STAT_ROWS = 16
CHUNK = 2 * T + STAT_ROWS


def params(mib):
    return pltpu.CompilerParams(vmem_limit_bytes=mib * 2**20)


def cost(flops, moved, exps=0):
    return pl.CostEstimate(flops=flops, bytes_accessed=moved, transcendentals=exps)


def whole(shape):
    return pl.BlockSpec(shape, lambda *_: (0,) * len(shape))


def prep_kernel(key_ref, ids_ref, weights_ref, lists_ref, picker_ref, combine_ref):
    key = key_ref[...]
    lane = lax.broadcasted_iota(jnp.int32, (T, 128), 1)
    columns = [jnp.broadcast_to(key[:, j : j + 1], (T, 128)) for j in range(key.shape[1])]
    for c in range(NC):
        here = lane + c * 128
        hits = jnp.zeros((T, 128), F32)
        for column in columns:
            hits = hits + jnp.where(column == here, 1.0, 0.0)
        lists_ref[c] = hits.astype(BF)
    rows = NG * NC * CAPE
    place = lax.broadcasted_iota(jnp.int32, (T, rows), 1)
    expert = place // 16
    slot = (place % CAPE).astype(F32)
    taken = jnp.zeros((T, rows), F32)
    coefficient = jnp.zeros((T, rows), F32)
    for j in range(ids_ref.shape[1]):
        hit = jnp.broadcast_to(ids_ref[:, j : j + 1], (T, rows)) == expert
        taken = taken + jnp.where(hit, 1.0, 0.0)
        coefficient = coefficient + jnp.where(hit, jnp.broadcast_to(weights_ref[:, j : j + 1], (T, rows)), 0.0)
    before = (lax.broadcasted_iota(jnp.int32, (T, T), 1) < lax.broadcasted_iota(jnp.int32, (T, T), 0)).astype(F32)
    order = jnp.dot(before.astype(BF), taken.astype(BF), preferred_element_type=F32)
    hit = jnp.where((taken > 0.5) & (order == slot), 1.0, 0.0)
    picker_ref[...] = jnp.transpose(hit).astype(BF)
    table = hit * coefficient
    high = table.astype(BF)
    combine_ref[:T] = high
    combine_ref[T:] = (table - high.astype(F32)).astype(BF)


def resident_kernel(length_ref, start_ref, q_ref, k_ref, v_ref, out_ref, peak_ref, total_ref):
    step = pl.program_id(0)
    each = k_ref.shape[0]
    position = lax.broadcasted_iota(jnp.int32, (HEADS, 128), 1) + start_ref[0]
    for i in range(each):
        t = step * each + i
        valid = position < length_ref[t]
        scores = jnp.concatenate(
            [
                lax.dot_general(
                    q_ref[i, g * HPK : (g + 1) * HPK, :],
                    k_ref[i, :, g * HW : (g + 1) * HW],
                    NT,
                    preferred_element_type=F32,
                )
                for g in range(KV)
            ],
            axis=0,
        )
        scores = jnp.where(valid, scores * SCALE, NEG)
        peak = jnp.max(scores, axis=1, keepdims=True)
        weights = jnp.where(valid, jnp.exp(scores - peak), 0.0)
        total = jnp.sum(weights, axis=1, keepdims=True)
        rounded = weights.astype(BF)
        out = jnp.concatenate(
            [
                jnp.dot(
                    rounded[g * HPK : (g + 1) * HPK, :],
                    v_ref[i, :, g * HW : (g + 1) * HW],
                    preferred_element_type=F32,
                )
                for g in range(KV)
            ],
            axis=0,
        )
        here = pl.ds(t, HEADS, stride=T)
        out_ref[here, :] = out
        peak_ref[here, :] = jnp.broadcast_to(peak, (HEADS, 128))
        total_ref[here, :] = jnp.broadcast_to(total, (HEADS, 128))


def recalled_kernel(lists_ref, q_ref, pages_ref, out_res_ref, peak_res_ref, total_res_ref, send_ref):
    rows = HPK * T
    tokens = NG * SLOTS * TOK
    counts = jnp.sum(lists_ref[...].astype(F32), axis=0).astype(BF)
    spread = (
        lax.broadcasted_iota(jnp.int32, (128, tokens), 1) // TOK == lax.broadcasted_iota(jnp.int32, (128, tokens), 0)
    ).astype(F32)
    times = jnp.dot(counts, spread.astype(BF), preferred_element_type=F32)[None]
    keys = jnp.concatenate([pages_ref[b, :128, :] for b in range(NG)], axis=0)
    values = jnp.concatenate([pages_ref[b, 128:, :] for b in range(NG)], axis=0)
    scores = lax.dot_general(q_ref[...], keys, NT, preferred_element_type=F32)
    scores = jnp.where(times > 0.5, scores.reshape(HPK, T, tokens) * SCALE, NEG)
    peak_res = peak_res_ref[...]
    peak = jnp.max(scores, axis=2, keepdims=True).reshape(rows, 1)
    peak = jnp.maximum(jnp.broadcast_to(peak, (rows, 128)), peak_res)
    peak_high = peak.astype(BF).astype(F32)
    peak_low = (peak - peak_high).astype(BF).astype(F32)
    base = peak_high + peak_low
    weights = jnp.where(times > 0.5, jnp.exp(scores - base[:, :1].reshape(HPK, T, 1)) * times, 0.0)
    total = jnp.sum(weights, axis=2, keepdims=True).reshape(rows, 1)
    out = jnp.dot(weights.reshape(rows, tokens).astype(BF), values, preferred_element_type=F32)
    factor = jnp.exp(peak_res - base)
    out = out + factor * out_res_ref[...]
    total = jnp.broadcast_to(total, (rows, 128)) + factor * total_res_ref[...]
    total_high = total.astype(BF).astype(F32)
    total_low = total - total_high
    lane = lax.broadcasted_iota(jnp.int32, (rows, 128), 1) % 4
    stats = jnp.where(
        lane == 0, peak_high, jnp.where(lane == 1, peak_low, jnp.where(lane == 2, total_high, total_low))
    ).reshape(HPK // 2, 2, T, 128)
    lane = lax.broadcasted_iota(jnp.int32, (HPK // 2, T, 128), 2)
    stats = jnp.where(lane < 4, stats[:, 0], stats[:, 1])
    send_ref[:, : 2 * T, :] = out.reshape(HPK // 2, 2 * T, 128).astype(BF)
    send_ref[:, 2 * T :, :] = stats.astype(BF)


def project_kernel(parts_ref, weight_ref, send_ref):
    stats = parts_ref[:, 2 * T :, :].astype(F32)
    heads = []
    for i in range(2):
        peak = stats[:, :, 4 * i : 4 * i + 1] + stats[:, :, 4 * i + 1 : 4 * i + 2]
        total = stats[:, :, 4 * i + 2 : 4 * i + 3] + stats[:, :, 4 * i + 3 : 4 * i + 4]
        factor = jnp.exp(peak - jnp.max(peak, axis=0, keepdims=True))
        total = jnp.sum(factor * total, axis=0)
        out = jnp.sum(factor * parts_ref[:, i * T : (i + 1) * T, :].astype(F32), axis=0)
        heads.append((out / total).astype(BF))
    attention = jnp.concatenate(heads, axis=1)
    wide = 512
    for j in range(D // wide):
        block = jnp.dot(attention, weight_ref[:, j * wide : (j + 1) * wide], preferred_element_type=F32).astype(BF)
        for i in range(wide // 128):
            send_ref[j * (wide // 128) + i] = block[:, i * 128 : (i + 1) * 128]


def dispatch_kernel(sums_ref, residual_ref, picker_ref, hidden_ref, send_ref):
    hidden = residual_ref[...].astype(F32) + jnp.sum(sums_ref[...].astype(F32), axis=0)
    hidden_ref[...] = hidden
    send_ref[...] = jnp.dot(picker_ref[...], hidden.astype(BF), preferred_element_type=F32).astype(BF)


def expert_kernel(rows_ref, gain_ref, gate_ref, up_ref, down_ref, send_ref, wide_ref, token_ref):
    wide_ref[...] = rows_ref[...].astype(F32)
    for c in range(NC):
        for s in range(CAPE):
            token_ref[s * NG : (s + 1) * NG, c * 128 : (c + 1) * 128] = wide_ref[pl.ds(c * CAPE + s, NG, stride=128), :]
    hidden = token_ref[...]
    normed = (hidden * lax.rsqrt(jnp.mean(hidden * hidden, axis=1, keepdims=True) + EPS) * gain_ref[...]).astype(BF)
    gate = lax.dot_general(normed, gate_ref[...], NT, preferred_element_type=F32)
    up = lax.dot_general(normed, up_ref[...], NT, preferred_element_type=F32)
    act = (gate / (1.0 + jnp.exp(-gate)) * up).astype(BF)
    wide = 512
    for j in range(D // wide):
        block = jnp.dot(act, down_ref[:, j * wide : (j + 1) * wide], preferred_element_type=F32)
        for i in range(wide // 128):
            for s in range(CAPE):
                wide_ref[pl.ds((j * (wide // 128) + i) * CAPE + s, NG, stride=128), :] = block[
                    s * NG : (s + 1) * NG, i * 128 : (i + 1) * 128
                ]
    send_ref[...] = wide_ref[...].astype(BF)


def combine_kernel(rows_ref, table_ref, hidden_ref, out_ref):
    both = jnp.dot(table_ref[...], rows_ref[...], preferred_element_type=F32)
    out_ref[...] = (hidden_ref[...] + both[:T] + both[T:]).astype(BF)


def shards(
    queries,
    resident_key_cache,
    resident_value_cache,
    res_len,
    visual_page_pool,
    recall_holder,
    recall_slot,
    o_weight,
    residual,
    norm_gain,
    expert_ids,
    expert_weights,
    w_gate,
    w_up,
    w_down,
):
    ctx_index = lax.axis_index(CTX)
    rows = NG * NC * CAPE

    own_pages = jnp.swapaxes(visual_page_pool, 0, 1).reshape(2 * SLOTS * TOK, KV * HW)
    pages = lax.all_gather(own_pages, GRP)

    holder = recall_holder[0]
    key = (holder % NC) * 128 + (holder // NC) * SLOTS + recall_slot[0]
    lists, picker, table = pl.pallas_call(
        prep_kernel,
        out_shape=(
            jax.ShapeDtypeStruct((NC, T, 128), BF),
            jax.ShapeDtypeStruct((rows, T), BF),
            jax.ShapeDtypeStruct((2 * T, rows), BF),
        ),
        compiler_params=params(16),
        cost_estimate=cost(4_000_000, 400_000),
        name="prep",
    )(key, expert_ids, expert_weights)
    lists = lax.all_to_all(lists, CTX, split_axis=0, concat_axis=0, tiled=True)

    by_request = queries.reshape(T, HEADS, HW)
    by_head = jnp.swapaxes(by_request, 0, 1).reshape(HEADS * T, HW)
    each = 4
    stat = jax.ShapeDtypeStruct((HEADS * T, 128), F32)
    out_res, peak_res, total_res = pl.pallas_call(
        resident_kernel,
        grid=(T // each,),
        in_specs=[
            pl.BlockSpec(memory_space=pltpu.SMEM),
            pl.BlockSpec(memory_space=pltpu.SMEM),
            pl.BlockSpec((each, HEADS, HW), lambda i: (i, 0, 0)),
            pl.BlockSpec((each, 128, KV * HW), lambda i: (i, 0, 0)),
            pl.BlockSpec((each, 128, KV * HW), lambda i: (i, 0, 0)),
        ],
        out_specs=[whole((HEADS * T, 128))] * 3,
        out_shape=(stat, stat, stat),
        compiler_params=params(24),
        cost_estimate=cost(70_000_000, 6_000_000, 131_072),
        name="resident",
    )(res_len, (ctx_index * 128).reshape(1).astype(jnp.int32), by_request, resident_key_cache, resident_value_cache)

    block = pl.BlockSpec((HPK * T, 128), lambda k: (k, 0))
    parts = pl.pallas_call(
        recalled_kernel,
        grid=(KV,),
        in_specs=[
            whole((NC, T, 128)),
            block,
            pl.BlockSpec((NG, 256, 128), lambda k: (0, 0, k)),
            block,
            block,
            block,
        ],
        out_specs=pl.BlockSpec((HPK // 2, CHUNK, 128), lambda k: (k, 0, 0)),
        out_shape=jax.ShapeDtypeStruct((NC, CHUNK, 128), BF),
        compiler_params=params(40),
        cost_estimate=cost(550_000_000, 5_000_000, 1_048_576),
        name="recalled",
    )(lists, by_head, pages, out_res, peak_res, total_res)
    parts = lax.all_to_all(parts, CTX, split_axis=0, concat_axis=0, tiled=True)

    sums = pl.pallas_call(
        project_kernel,
        out_shape=jax.ShapeDtypeStruct((NC, T, 128), BF),
        compiler_params=params(24),
        cost_estimate=cost(40_000_000, 2_700_000, 2048),
        name="project",
    )(parts, o_weight)
    sums = lax.all_to_all(sums, CTX, split_axis=0, concat_axis=0, tiled=True)

    own_residual = lax.dynamic_slice_in_dim(residual, ctx_index * 128, 128, 1)
    hidden, send = pl.pallas_call(
        dispatch_kernel,
        out_shape=(jax.ShapeDtypeStruct((T, 128), F32), jax.ShapeDtypeStruct((rows, 128), BF)),
        compiler_params=params(16),
        cost_estimate=cost(4_000_000, 500_000),
        name="dispatch",
    )(sums, own_residual, picker)
    arrived = lax.all_to_all(send.reshape(NG * NC, CAPE, 128), ALL, split_axis=0, concat_axis=0, tiled=True)

    results = pl.pallas_call(
        expert_kernel,
        out_shape=jax.ShapeDtypeStruct((rows, 128), BF),
        scratch_shapes=[pltpu.VMEM((rows, 128), F32), pltpu.VMEM((NG * CAPE, D), F32)],
        compiler_params=params(32),
        cost_estimate=cost(160_000_000, 5_300_000, 8192),
        name="experts",
    )(arrived.reshape(rows, 128), norm_gain.reshape(1, D), w_gate[0], w_up[0], w_down[0])
    returned = lax.all_to_all(results.reshape(NG * NC, CAPE, 128), ALL, split_axis=0, concat_axis=0, tiled=True)

    return pl.pallas_call(
        combine_kernel,
        out_shape=jax.ShapeDtypeStruct((T, 128), BF),
        compiler_params=params(16),
        cost_estimate=cost(8_000_000, 400_000),
        name="combine",
    )(returned.reshape(rows, 128), table, hidden)


def solution(mesh):
    fine = Mesh(mesh.devices.reshape(4, 2, 4, 8), ALL)
    placed = (
        P(GRP, None),
        P(GRP, CTX, None),
        P(GRP, CTX, None),
        P(GRP),
        P(ALL, None, None, None),
        P(CTX, GRP, None),
        P(CTX, GRP, None),
        P(CTX, None),
        P(GRP, None),
        P(),
        P(GRP, None),
        P(GRP, None),
        P(ALL, None, None),
        P(ALL, None, None),
        P(ALL, None, None),
    )
    return jax.shard_map(shards, mesh=fine, in_specs=placed, out_specs=P(GRP, CTX), check_vma=False)
```

```python
import functools

import jax
import jax.numpy as jnp
from jax import lax
from jax.experimental import pallas as pl
from jax.experimental.pallas import tpu as pltpu
from jax.sharding import Mesh, PartitionSpec as P

HEADS = 64
KV = 4
HPK = HEADS // KV
HW = 128
T = 16
D = 4096
NC = 32
NG = 8
CAPE = 4
FP = 192
TOK = 8
SLOTS = 16
EPS = 1e-06
NEG = -(2.0**100)
SCALE = HW**-0.5
BF = jnp.bfloat16
F32 = jnp.float32
GRP = ("y", "core")
CTX = ("x", "z")
ALL = GRP + CTX
NT = (((1,), (1,)), ((), ()))
STAT_ROWS = 16
EACH = 4
CHUNK = 2 * T + STAT_ROWS


def params(mib):
    return pltpu.CompilerParams(vmem_limit_bytes=mib * 2**20)


def cost(flops, moved, exps=0):
    return pl.CostEstimate(flops=flops, bytes_accessed=moved, transcendentals=exps)


def lists_kernel(key_ref, lists_ref):
    key = key_ref[...]
    lane = lax.broadcasted_iota(jnp.int32, (T, 128), 1)
    columns = [jnp.broadcast_to(key[:, j : j + 1], (T, 128)) - lane for j in range(key.shape[1])]
    for c in range(NC):
        hits = [column == c * 128 for column in columns]
        while len(hits) > 1:
            hits = [hits[i] | hits[i + 1] for i in range(0, len(hits), 2)]
        lists_ref[c] = jnp.where(hits[0], 1.0, 0.0).astype(BF)


def prepare_kernel(ids_ref, weights_ref, picker_ref, combine_ref):
    rows = NG * NC * CAPE
    one = (lax.broadcasted_iota(jnp.int32, (T, T), 1) == lax.broadcasted_iota(jnp.int32, (T, T), 0)).astype(F32)
    exact = dict(preferred_element_type=F32, precision=lax.Precision.HIGHEST)
    ids = lax.dot_general(one, ids_ref[...].astype(F32), NT, **exact)
    weights = lax.dot_general(one, weights_ref[...], NT, **exact)
    place = lax.broadcasted_iota(jnp.int32, (T, rows), 1)
    expert = (place // 16).astype(F32)
    slot = (place % CAPE).astype(F32)
    taken = jnp.zeros((T, rows), F32)
    coefficient = jnp.zeros((T, rows), F32)
    for j in range(ids_ref.shape[0]):
        hit = jnp.abs(jnp.broadcast_to(ids[:, j : j + 1], (T, rows)) - expert) < 0.5
        taken = taken + jnp.where(hit, 1.0, 0.0)
        coefficient = coefficient + jnp.where(hit, jnp.broadcast_to(weights[:, j : j + 1], (T, rows)), 0.0)
    before = (lax.broadcasted_iota(jnp.int32, (T, T), 1) < lax.broadcasted_iota(jnp.int32, (T, T), 0)).astype(F32)
    order = jnp.dot(before.astype(BF), taken.astype(BF), preferred_element_type=F32)
    hit = jnp.where((taken > 0.5) & (order == slot), 1.0, 0.0)
    picker_ref[...] = hit.astype(BF)
    table = hit * coefficient
    high = table.astype(BF)
    combine_ref[:T] = high
    combine_ref[T:] = (table - high.astype(F32)).astype(BF)


def resident_kernel(length_ref, start_ref, q, k, v, out_ref, stats_ref, wide):
    steps = k.shape[0] // EACH
    for h in range(HEADS):
        head = q[:, h * HW : (h + 1) * HW]
        wide[h * T : (h + 1) * T, :] = head.astype(F32)

    position = lax.broadcasted_iota(jnp.int32, (HEADS, 128), 1) + start_ref[0]
    lane = lax.broadcasted_iota(jnp.int32, (HEADS, 128), 1)
    pairs = [(i, g) for i in range(EACH) for g in range(KV)]

    @pl.loop(0, steps)
    def _(step):
        base = step * EACH
        own = [wide[pl.ds(base + i, HEADS, stride=T), :].astype(BF) for i in range(EACH)]
        scores = [
            lax.dot_general(
                own[i][g * HPK : (g + 1) * HPK], k[base + i, :, g * HW : (g + 1) * HW], NT, preferred_element_type=F32
            )
            for i, g in pairs
        ]
        scores = jnp.concatenate(scores, axis=0).reshape(EACH, HEADS, 128)
        valid = [position < length_ref[base + i] for i in range(EACH)]
        scores = jnp.stack([jnp.where(valid[i], scores[i] * SCALE, NEG) for i in range(EACH)])
        peak = jnp.max(scores, axis=2, keepdims=True)
        chances = jnp.exp(scores - peak)
        chances = jnp.stack([jnp.where(valid[i], chances[i], 0.0) for i in range(EACH)])
        total = jnp.sum(chances, axis=2, keepdims=True)
        rounded = chances.astype(BF)
        out = [
            jnp.dot(
                rounded[i, g * HPK : (g + 1) * HPK],
                v[base + i, :, g * HW : (g + 1) * HW],
                preferred_element_type=F32,
            )
            for i, g in pairs
        ]
        for i in range(EACH):
            here = pl.ds(base + i, HEADS, stride=T)
            out_ref[here, :] = jnp.concatenate(out[i * KV : (i + 1) * KV], axis=0)
            stats_ref[here, :] = jnp.where(lane < 64, peak[i], total[i])


def recalled_kernel(half, lists_ref, q_ref, *refs):
    pages, (out_ref, stats_ref, *given) = refs[: NG // 2], refs[NG // 2 :]
    rows = HPK * T
    tokens = len(pages) * SLOTS * TOK
    counts = jnp.sum(lists_ref[...].astype(F32), axis=0).astype(BF)
    spread = (
        lax.broadcasted_iota(jnp.int32, (128, tokens), 1) // TOK + half * (tokens // TOK)
        == lax.broadcasted_iota(jnp.int32, (128, tokens), 0)
    ).astype(F32)
    times = jnp.dot(counts, spread.astype(BF), preferred_element_type=F32)
    bias = jnp.where(times > 0.5, 0.0, NEG)[None]
    times = times[None]
    lanes = lax.broadcasted_iota(jnp.int32, (rows, 128), 1)
    kind = lanes % 4
    lane = lax.broadcasted_iota(jnp.int32, (HPK // 2, T, 128), 2)
    for g in range(KV):
        own = slice(g * rows, (g + 1) * rows)
        columns = slice(g * HW, (g + 1) * HW)
        keys, values = [
            jnp.concatenate([ref[p, m, :, columns] for ref in pages for p in range(SLOTS)], axis=0) for m in range(2)
        ]
        heads = range(g * HPK, (g + 1) * HPK)
        queries = jnp.concatenate([q_ref[:, h * HW : (h + 1) * HW] for h in heads], axis=0)
        scores = lax.dot_general(queries, keys, NT, preferred_element_type=F32)
        scores = scores.reshape(HPK, T, tokens) * SCALE + bias
        stats = stats_ref[own, :]
        before = jnp.broadcast_to(stats[:, :1], (rows, 128))
        peak = jnp.max(scores, axis=2, keepdims=True).reshape(rows, 1)
        peak = jnp.maximum(jnp.broadcast_to(peak, (rows, 128)), before)
        if half:
            peak_high = peak.astype(BF).astype(F32)
            peak_low = (peak - peak_high).astype(BF).astype(F32)
            base = peak_high + peak_low
        else:
            base = peak
        weights = jnp.exp(scores - base[:, :1].reshape(HPK, T, 1)) * times
        total = jnp.sum(weights, axis=2, keepdims=True).reshape(rows, 1)
        out = jnp.dot(weights.reshape(rows, tokens).astype(BF), values, preferred_element_type=F32)
        factor = jnp.exp(before - base)
        out = out + factor * out_ref[own, :]
        total = jnp.broadcast_to(total, (rows, 128)) + factor * jnp.broadcast_to(stats[:, 64:65], (rows, 128))
        if not half:
            given[0][own, :] = out
            given[1][own, :] = jnp.where(lanes < 64, base, total)
            continue
        total_high = total.astype(BF).astype(F32)
        stats = jnp.where(
            kind == 0, peak_high, jnp.where(kind == 1, peak_low, jnp.where(kind == 2, total_high, total - total_high))
        ).reshape(HPK // 2, 2, T, 128)
        here = slice(g * (HPK // 2), (g + 1) * (HPK // 2))
        given[0][here, : 2 * T, :] = out.reshape(HPK // 2, 2 * T, 128).astype(BF)
        given[0][here, 2 * T :, :] = jnp.where(lane < 4, stats[:, 0], stats[:, 1]).astype(BF)


def project_kernel(parts_ref, weight_ref, send_ref):
    stats = parts_ref[:, 2 * T :, :].astype(F32)
    heads = []
    for i in range(2):
        peak = stats[:, :, 4 * i : 4 * i + 1] + stats[:, :, 4 * i + 1 : 4 * i + 2]
        total = stats[:, :, 4 * i + 2 : 4 * i + 3] + stats[:, :, 4 * i + 3 : 4 * i + 4]
        factor = jnp.exp(peak - jnp.max(peak, axis=0, keepdims=True))
        total = jnp.sum(factor * total, axis=0)
        out = jnp.sum(factor * parts_ref[:, i * T : (i + 1) * T, :].astype(F32), axis=0)
        heads.append((out / total).astype(BF))
    attention = jnp.concatenate(heads, axis=1)
    wide = 512
    for j in range(D // wide):
        block = jnp.dot(attention, weight_ref[:, j * wide : (j + 1) * wide], preferred_element_type=F32).astype(BF)
        for i in range(wide // 128):
            send_ref[j * (wide // 128) + i] = block[:, i * 128 : (i + 1) * 128]


def dispatch_kernel(sums_ref, residual_ref, picker_ref, hidden_ref, send_ref):
    hidden = residual_ref[...].astype(F32) + jnp.sum(sums_ref[...].astype(F32), axis=0)
    hidden_ref[...] = hidden
    send_ref[...] = lax.dot_general(
        picker_ref[...], hidden.astype(BF), (((0,), (0,)), ((), ())), preferred_element_type=F32
    ).astype(BF)


def expert_kernel(rows_ref, gain_ref, gate_ref, up_ref, down_hbm, send_ref, wide_ref, token_ref, down_ref, sem):
    late = pltpu.make_async_copy(down_hbm, down_ref, sem)
    late.start()
    wide_ref[...] = rows_ref[...].astype(F32)
    for c in range(NC):
        for s in range(CAPE):
            token_ref[s * NG : (s + 1) * NG, c * 128 : (c + 1) * 128] = wide_ref[pl.ds(c * CAPE + s, NG, stride=128), :]
    hidden = token_ref[...]
    normed = (hidden * lax.rsqrt(jnp.mean(hidden * hidden, axis=1, keepdims=True) + EPS) * gain_ref[...]).astype(BF)
    gate = lax.dot_general(normed, gate_ref[...], NT, preferred_element_type=F32)
    up = lax.dot_general(normed, up_ref[...], NT, preferred_element_type=F32)
    act = (gate / (1.0 + jnp.exp(-gate)) * up).astype(BF)
    wide = 512
    late.wait()
    for j in range(D // wide):
        block = jnp.dot(act, down_ref[:, j * wide : (j + 1) * wide], preferred_element_type=F32)
        for i in range(wide // 128):
            for s in range(CAPE):
                wide_ref[pl.ds((j * (wide // 128) + i) * CAPE + s, NG, stride=128), :] = block[
                    s * NG : (s + 1) * NG, i * 128 : (i + 1) * 128
                ]
    send_ref[...] = wide_ref[...].astype(BF)


def combine_kernel(rows_ref, table_ref, hidden_ref, out_ref):
    both = jnp.dot(table_ref[...], rows_ref[...], preferred_element_type=F32)
    out_ref[...] = (hidden_ref[...] + both[:T] + both[T:]).astype(BF)


def shards(
    queries,
    resident_key_cache,
    resident_value_cache,
    res_len,
    visual_page_pool,
    recall_holder,
    recall_slot,
    o_weight,
    residual,
    norm_gain,
    expert_ids,
    expert_weights,
    w_gate,
    w_up,
    w_down,
):
    ctx_index = lax.axis_index(CTX)
    rows = NG * NC * CAPE

    smem = pl.BlockSpec(memory_space=pltpu.SMEM)
    vmem = pl.BlockSpec(memory_space=pltpu.VMEM)
    hbm = pl.BlockSpec(memory_space=pltpu.HBM)
    pages = [visual_page_pool]
    for k in range(1, 4):
        pages.append(lax.ppermute(visual_page_pool, "y", [(i, (i + k) % 4) for i in range(4)]))
    pages += [lax.ppermute(part, "core", [(0, 1), (1, 0)]) for part in pages]

    holder = recall_holder[0]
    group = holder // NC
    back = (lax.axis_index("y") + 4 - group // 2) % 4
    near = jnp.where(group % 2 == lax.axis_index("core"), back, back + 4)
    key = (holder % NC) * 128 + near * SLOTS + recall_slot[0]
    lists = pl.pallas_call(
        lists_kernel,
        out_shape=jax.ShapeDtypeStruct((NC, T, 128), BF),
        compiler_params=params(4),
        cost_estimate=cost(4_000_000, 140_000),
        name="lists",
    )(key)
    lists = lax.all_to_all(lists, CTX, split_axis=0, concat_axis=0, tiled=True)

    wide = jax.ShapeDtypeStruct((HEADS * T, 128), F32)
    out, stats = pl.pallas_call(
        resident_kernel,
        in_specs=[smem, smem, vmem, vmem, vmem],
        out_shape=(wide, wide),
        scratch_shapes=[pltpu.VMEM((HEADS * T, HW), F32)],
        compiler_params=params(12),
        cost_estimate=cost(70_000_000, 6_000_000, 131_072),
        name="resident",
    )(res_len, (ctx_index * 128).reshape(1).astype(jnp.int32), queries, resident_key_cache, resident_value_cache)

    for half in range(2):
        last = half == 1
        result = pl.pallas_call(
            functools.partial(recalled_kernel, half),
            out_shape=jax.ShapeDtypeStruct((NC, CHUNK, 128), BF) if last else (wide, wide),
            compiler_params=params(16),
            cost_estimate=cost(270_000_000, 4_000_000, 524_288),
            name="recalled",
        )(lists, queries, *pages[half * 4 : half * 4 + 4], out, stats)
        if not last:
            out, stats = result
    parts = result
    parts = lax.all_to_all(parts, CTX, split_axis=0, concat_axis=0, tiled=True)

    sums = pl.pallas_call(
        project_kernel,
        out_shape=jax.ShapeDtypeStruct((NC, T, 128), BF),
        compiler_params=params(8),
        cost_estimate=cost(40_000_000, 2_700_000, 2048),
        name="project",
    )(parts, o_weight)
    ids, chances, _ = lax.optimization_barrier((expert_ids.T, expert_weights.T, sums))
    picker, table = pl.pallas_call(
        prepare_kernel,
        out_shape=(jax.ShapeDtypeStruct((T, rows), BF), jax.ShapeDtypeStruct((2 * T, rows), BF)),
        compiler_params=params(4),
        cost_estimate=cost(4_000_000, 200_000),
        name="prepare",
    )(ids, chances)
    sums = lax.all_to_all(sums, CTX, split_axis=0, concat_axis=0, tiled=True)

    own_residual = lax.dynamic_slice_in_dim(residual, ctx_index * 128, 128, 1)
    hidden, send = pl.pallas_call(
        dispatch_kernel,
        out_shape=(jax.ShapeDtypeStruct((T, 128), F32), jax.ShapeDtypeStruct((rows, 128), BF)),
        compiler_params=params(8),
        cost_estimate=cost(4_000_000, 500_000),
        name="dispatch",
    )(sums, own_residual, picker)
    arrived = lax.all_to_all(send.reshape(NG * NC, CAPE, 128), ALL, split_axis=0, concat_axis=0, tiled=True)

    results = pl.pallas_call(
        expert_kernel,
        in_specs=[vmem, vmem, vmem, vmem, hbm],
        out_shape=jax.ShapeDtypeStruct((rows, 128), BF),
        scratch_shapes=[pltpu.VMEM((rows, 128), F32), pltpu.VMEM((NG * CAPE, D), F32), pltpu.VMEM((FP, D), BF), pltpu.SemaphoreType.DMA(())],
        compiler_params=params(12),
        cost_estimate=cost(160_000_000, 5_300_000, 8192),
        name="experts",
    )(arrived.reshape(rows, 128), norm_gain.reshape(1, D), w_gate[0], w_up[0], w_down[0])
    returned = lax.all_to_all(results.reshape(NG * NC, CAPE, 128), ALL, split_axis=0, concat_axis=0, tiled=True)

    return pl.pallas_call(
        combine_kernel,
        out_shape=jax.ShapeDtypeStruct((T, 128), BF),
        compiler_params=params(8),
        cost_estimate=cost(8_000_000, 400_000),
        name="combine",
    )(returned.reshape(rows, 128), table, hidden)


def solution(mesh):
    fine = Mesh(mesh.devices.reshape(4, 2, 4, 8), ALL)
    placed = (
        P(GRP, None),
        P(GRP, CTX, None),
        P(GRP, CTX, None),
        P(GRP),
        P(ALL, None, None, None),
        P(CTX, GRP, None),
        P(CTX, GRP, None),
        P(CTX, None),
        P(GRP, None),
        P(),
        P(GRP, None),
        P(GRP, None),
        P(ALL, None, None),
        P(ALL, None, None),
        P(ALL, None, None),
    )
    return jax.shard_map(shards, mesh=fine, in_specs=placed, out_specs=P(GRP, CTX), check_vma=False)
```

```python
import functools

import jax
import jax.numpy as jnp
from jax import lax
from jax.experimental import pallas as pl
from jax.experimental.pallas import tpu as pltpu
from jax.sharding import Mesh, PartitionSpec as P

HEADS = 64
KV = 4
HPK = HEADS // KV
HW = 128
T = 16
D = 4096
NC = 32
NG = 8
CAPE = 4
FP = 192
TOK = 8
SLOTS = 16
EPS = 1e-06
NEG = -(2.0**100)
SCALE = HW**-0.5
BF = jnp.bfloat16
F32 = jnp.float32
GRP = ("y", "core")
CTX = ("x", "z")
ALL = GRP + CTX
NT = (((1,), (1,)), ((), ()))
STAT_ROWS = 8
EACH = 4
CHUNK = 2 * T + STAT_ROWS


def params(mib):
    return pltpu.CompilerParams(vmem_limit_bytes=mib * 2**20)


def cost(flops, moved, exps=0):
    return pl.CostEstimate(flops=flops, bytes_accessed=moved, transcendentals=exps)


def lists_kernel(key_ref, lists_ref):
    key = key_ref[...]
    lane = lax.broadcasted_iota(jnp.int32, (T, 128), 1)
    columns = [jnp.broadcast_to(key[:, j : j + 1], (T, 128)) - lane for j in range(key.shape[1])]
    for c in range(NC):
        hits = [column == c * 128 for column in columns]
        while len(hits) > 1:
            hits = [hits[i] | hits[i + 1] for i in range(0, len(hits), 2)]
        lists_ref[c] = jnp.where(hits[0], 1.0, 0.0).astype(BF)


def prepare_kernel(ids_ref, weights_ref, picker_ref, combine_ref):
    rows = NG * NC * CAPE
    one = (lax.broadcasted_iota(jnp.int32, (T, T), 1) == lax.broadcasted_iota(jnp.int32, (T, T), 0)).astype(F32)
    exact = dict(preferred_element_type=F32, precision=lax.Precision.HIGHEST)
    ids = lax.dot_general(one, ids_ref[...].astype(F32), NT, **exact)
    weights = lax.dot_general(one, weights_ref[...], NT, **exact)
    place = lax.broadcasted_iota(jnp.int32, (T, rows), 1)
    expert = (place // 16).astype(F32)
    slot = (place % CAPE).astype(F32)
    taken = jnp.zeros((T, rows), F32)
    coefficient = jnp.zeros((T, rows), F32)
    for j in range(ids_ref.shape[0]):
        hit = jnp.abs(jnp.broadcast_to(ids[:, j : j + 1], (T, rows)) - expert) < 0.5
        taken = taken + jnp.where(hit, 1.0, 0.0)
        coefficient = coefficient + jnp.where(hit, jnp.broadcast_to(weights[:, j : j + 1], (T, rows)), 0.0)
    before = (lax.broadcasted_iota(jnp.int32, (T, T), 1) < lax.broadcasted_iota(jnp.int32, (T, T), 0)).astype(F32)
    order = jnp.dot(before.astype(BF), taken.astype(BF), preferred_element_type=F32)
    hit = jnp.where((taken > 0.5) & (order == slot), 1.0, 0.0)
    picker_ref[...] = hit.astype(BF)
    table = hit * coefficient
    high = table.astype(BF)
    combine_ref[:T] = high
    combine_ref[T:] = (table - high.astype(F32)).astype(BF)


def resident_kernel(length_ref, start_ref, q_hbm, keys_hbm, values_hbm, out_ref, stats_ref, wide, q, k, v, sems):
    steps = k.shape[0] // EACH
    first = pltpu.make_async_copy(q_hbm, q, sems.at[2 * steps])
    first.start()

    def chunk(i):
        here = pl.ds(i * EACH, EACH)
        return (
            pltpu.make_async_copy(keys_hbm.at[here], k.at[here], sems.at[2 * i]),
            pltpu.make_async_copy(values_hbm.at[here], v.at[here], sems.at[2 * i + 1]),
        )

    for i in range(steps):
        for copy in chunk(i):
            copy.start()
    first.wait()
    for h in range(HEADS):
        head = q[:, h * HW : (h + 1) * HW]
        wide[h * T : (h + 1) * T, :] = head.astype(F32)

    position = lax.broadcasted_iota(jnp.int32, (HEADS, 128), 1) + start_ref[0]
    lane = lax.broadcasted_iota(jnp.int32, (HEADS, 128), 1)
    pairs = [(i, g) for i in range(EACH) for g in range(KV)]

    @pl.loop(0, steps)
    def _(step):
        for copy in chunk(step):
            copy.wait()
        base = step * EACH
        own = [wide[pl.ds(base + i, HEADS, stride=T), :].astype(BF) for i in range(EACH)]
        scores = [
            lax.dot_general(
                own[i][g * HPK : (g + 1) * HPK], k[base + i, :, g * HW : (g + 1) * HW], NT, preferred_element_type=F32
            )
            for i, g in pairs
        ]
        scores = jnp.concatenate(scores, axis=0).reshape(EACH, HEADS, 128)
        valid = [position < length_ref[base + i] for i in range(EACH)]
        scores = jnp.stack([jnp.where(valid[i], scores[i] * SCALE, NEG) for i in range(EACH)])
        peak = jnp.max(scores, axis=2, keepdims=True)
        chances = jnp.exp(scores - peak)
        chances = jnp.stack([jnp.where(valid[i], chances[i], 0.0) for i in range(EACH)])
        total = jnp.sum(chances, axis=2, keepdims=True)
        rounded = chances.astype(BF)
        out = [
            jnp.dot(
                rounded[i, g * HPK : (g + 1) * HPK],
                v[base + i, :, g * HW : (g + 1) * HW],
                preferred_element_type=F32,
            )
            for i, g in pairs
        ]
        for i in range(EACH):
            here = pl.ds(base + i, HEADS, stride=T)
            out_ref[here, :] = jnp.concatenate(out[i * KV : (i + 1) * KV], axis=0)
            stats_ref[here, :] = jnp.where(lane < 64, peak[i], total[i])


def recalled_kernel(half, lists_ref, q_ref, *refs):
    pages, given = refs[: NG // 2], refs[NG // 2 :]
    earlier, given = given[: 4 * half], given[4 * half :]
    rows = HPK * T
    tokens = len(pages) * SLOTS * TOK
    counts = jnp.sum(lists_ref[...].astype(F32), axis=0).astype(BF)
    spread = (
        lax.broadcasted_iota(jnp.int32, (128, tokens), 1) // TOK + half * (tokens // TOK)
        == lax.broadcasted_iota(jnp.int32, (128, tokens), 0)
    ).astype(F32)
    times = jnp.dot(counts, spread.astype(BF), preferred_element_type=F32)
    bias = jnp.where(times > 0.5, 0.0, NEG)[None]
    times = times[None]
    lanes = lax.broadcasted_iota(jnp.int32, (rows, 128), 1)
    kind = lanes % 4
    lane = lax.broadcasted_iota(jnp.int32, (HPK // 2, 8, 128), 2)
    for g in range(KV):
        own = slice(g * rows, (g + 1) * rows)
        columns = slice(g * HW, (g + 1) * HW)
        keys, values = [
            jnp.concatenate([ref[p, m, :, columns] for ref in pages for p in range(SLOTS)], axis=0) for m in range(2)
        ]
        heads = range(g * HPK, (g + 1) * HPK)
        queries = jnp.concatenate([q_ref[:, h * HW : (h + 1) * HW] for h in heads], axis=0)
        scores = lax.dot_general(queries, keys, NT, preferred_element_type=F32)
        scores = scores.reshape(HPK, T, tokens) * SCALE + bias
        peak = jnp.max(scores, axis=2, keepdims=True).reshape(rows, 1)
        peak = jnp.broadcast_to(peak, (rows, 128))
        joined = [(o[own, :], s[own, :]) for o, s in zip(earlier[::2], earlier[1::2], strict=True)]
        joined = [(o, jnp.broadcast_to(s[:, :1], (rows, 128)), s[:, 64:65]) for o, s in joined]
        for _, before, _ in joined:
            peak = jnp.maximum(peak, before)
        if half:
            peak_high = peak.astype(BF).astype(F32)
            peak_low = (peak - peak_high).astype(BF).astype(F32)
            base = peak_high + peak_low
        else:
            base = peak
        weights = jnp.exp(scores - base[:, :1].reshape(HPK, T, 1)) * times
        total = jnp.sum(weights, axis=2, keepdims=True).reshape(rows, 1)
        total = jnp.broadcast_to(total, (rows, 128))
        out = jnp.dot(weights.reshape(rows, tokens).astype(BF), values, preferred_element_type=F32)
        for o, before, t in joined:
            factor = jnp.exp(before - base)
            out = out + factor * o
            total = total + factor * jnp.broadcast_to(t, (rows, 128))
        if not half:
            given[0][own, :] = out
            given[1][own, :] = jnp.where(lanes < 64, base, total)
            continue
        total_high = total.astype(BF).astype(F32)
        stats = jnp.where(
            kind == 0, peak_high, jnp.where(kind == 1, peak_low, jnp.where(kind == 2, total_high, total - total_high))
        ).reshape(HPK // 2, 2, 2, 8, 128)
        here = slice(g * (HPK // 2), (g + 1) * (HPK // 2))
        given[0][here, : 2 * T, :] = out.reshape(HPK // 2, 2 * T, 128).astype(BF)
        stats = [jnp.where(lane < 4 + b, stats[:, 0, i], stats[:, 1, i]) for i, b in enumerate((0, 8))]
        given[0][here, 2 * T :, :] = jnp.where(lane < 8, *stats).astype(BF)


def project_kernel(parts_ref, weight_ref, send_ref):
    stats = parts_ref[:, 2 * T :, :].astype(F32)
    heads = []
    for i in range(2):
        high, low, total, rest = [
            jnp.concatenate([stats[:, :, 8 * b + 4 * i + q : 8 * b + 4 * i + q + 1] for b in range(2)], axis=1)
            for q in range(4)
        ]
        peak = high + low
        total = total + rest
        factor = jnp.exp(peak - jnp.max(peak, axis=0, keepdims=True))
        total = jnp.sum(factor * total, axis=0)
        out = jnp.sum(factor * parts_ref[:, i * T : (i + 1) * T, :].astype(F32), axis=0)
        heads.append((out / total).astype(BF))
    attention = jnp.concatenate(heads, axis=1)
    wide = 512
    for j in range(D // wide):
        block = jnp.dot(attention, weight_ref[:, j * wide : (j + 1) * wide], preferred_element_type=F32).astype(BF)
        for i in range(wide // 128):
            send_ref[j * (wide // 128) + i] = block[:, i * 128 : (i + 1) * 128]


def dispatch_kernel(sums_ref, residual_ref, picker_ref, hidden_ref, send_ref):
    hidden = residual_ref[...].astype(F32) + jnp.sum(sums_ref[...].astype(F32), axis=0)
    hidden_ref[...] = hidden
    send_ref[...] = lax.dot_general(
        picker_ref[...], hidden.astype(BF), (((0,), (0,)), ((), ())), preferred_element_type=F32
    ).astype(BF)


def expert_kernel(rows_ref, gain_ref, gate_ref, up_ref, down_hbm, send_ref, wide_ref, token_ref, down_ref, sem):
    late = pltpu.make_async_copy(down_hbm, down_ref, sem)
    late.start()
    wide_ref[...] = rows_ref[...].astype(F32)
    for c in range(NC):
        for s in range(CAPE):
            token_ref[s * NG : (s + 1) * NG, c * 128 : (c + 1) * 128] = wide_ref[pl.ds(c * CAPE + s, NG, stride=128), :]
    hidden = token_ref[...]
    normed = (hidden * lax.rsqrt(jnp.mean(hidden * hidden, axis=1, keepdims=True) + EPS) * gain_ref[...]).astype(BF)
    gate = lax.dot_general(normed, gate_ref[...], NT, preferred_element_type=F32)
    up = lax.dot_general(normed, up_ref[...], NT, preferred_element_type=F32)
    act = (gate / (1.0 + jnp.exp(-gate)) * up).astype(BF)
    wide = 512
    late.wait()
    for j in range(D // wide):
        block = jnp.dot(act, down_ref[:, j * wide : (j + 1) * wide], preferred_element_type=F32)
        for i in range(wide // 128):
            for s in range(CAPE):
                wide_ref[pl.ds((j * (wide // 128) + i) * CAPE + s, NG, stride=128), :] = block[
                    s * NG : (s + 1) * NG, i * 128 : (i + 1) * 128
                ]
    send_ref[...] = wide_ref[...].astype(BF)


def combine_kernel(rows_ref, table_ref, hidden_ref, out_ref):
    both = jnp.dot(table_ref[...], rows_ref[...], preferred_element_type=F32)
    out_ref[...] = (hidden_ref[...] + both[:T] + both[T:]).astype(BF)


def shards(
    queries,
    resident_key_cache,
    resident_value_cache,
    res_len,
    visual_page_pool,
    recall_holder,
    recall_slot,
    o_weight,
    residual,
    norm_gain,
    expert_ids,
    expert_weights,
    w_gate,
    w_up,
    w_down,
):
    ctx_index = lax.axis_index(CTX)
    rows = NG * NC * CAPE

    smem = pl.BlockSpec(memory_space=pltpu.SMEM)
    vmem = pl.BlockSpec(memory_space=pltpu.VMEM)
    hbm = pl.BlockSpec(memory_space=pltpu.HBM)
    pages = [visual_page_pool]
    for k in range(1, 4):
        pages.append(lax.ppermute(visual_page_pool, "y", [(i, (i + k) % 4) for i in range(4)]))
    pages += [lax.ppermute(part, "core", [(0, 1), (1, 0)]) for part in pages]

    holder = recall_holder[0]
    group = holder // NC
    back = (lax.axis_index("y") + 4 - group // 2) % 4
    near = jnp.where(group % 2 == lax.axis_index("core"), back, back + 4)
    key = (holder % NC) * 128 + near * SLOTS + recall_slot[0]
    lists = pl.pallas_call(
        lists_kernel,
        out_shape=jax.ShapeDtypeStruct((NC, T, 128), BF),
        compiler_params=params(4),
        cost_estimate=cost(4_000_000, 140_000),
        name="lists",
    )(key)
    lists = lax.all_to_all(lists, CTX, split_axis=0, concat_axis=0, tiled=True)

    wide = jax.ShapeDtypeStruct((HEADS * T, 128), F32)
    out, stats = pl.pallas_call(
        resident_kernel,
        in_specs=[smem, smem, hbm, hbm, hbm],
        out_shape=(wide, wide),
        scratch_shapes=[
            pltpu.VMEM((HEADS * T, HW), F32),
            pltpu.VMEM((T, HEADS * HW), BF),
            pltpu.VMEM((T, 128, KV * HW), BF),
            pltpu.VMEM((T, 128, KV * HW), BF),
            pltpu.SemaphoreType.DMA((2 * T // EACH + 1,)),
        ],
        compiler_params=params(51),
        cost_estimate=cost(70_000_000, 6_000_000, 131_072),
        name="resident",
    )(res_len, (ctx_index * 128).reshape(1).astype(jnp.int32), queries, resident_key_cache, resident_value_cache)

    own = pl.pallas_call(
        functools.partial(recalled_kernel, 0),
        out_shape=(wide, wide),
        compiler_params=params(16),
        cost_estimate=cost(270_000_000, 4_000_000, 524_288),
        name="recalled_own",
    )(lists, queries, *pages[:4])
    parts = pl.pallas_call(
        functools.partial(recalled_kernel, 1),
        out_shape=jax.ShapeDtypeStruct((NC, CHUNK, 128), BF),
        compiler_params=params(16),
        cost_estimate=cost(270_000_000, 4_000_000, 524_288),
        name="recalled_other",
    )(lists, queries, *pages[4:], *own, out, stats)
    parts = lax.all_to_all(parts, CTX, split_axis=0, concat_axis=0, tiled=True)

    sums = pl.pallas_call(
        project_kernel,
        out_shape=jax.ShapeDtypeStruct((NC, T, 128), BF),
        compiler_params=params(8),
        cost_estimate=cost(40_000_000, 2_700_000, 2048),
        name="project",
    )(parts, o_weight)
    ids, chances, _ = lax.optimization_barrier((expert_ids.T, expert_weights.T, sums))
    picker, table = pl.pallas_call(
        prepare_kernel,
        out_shape=(jax.ShapeDtypeStruct((T, rows), BF), jax.ShapeDtypeStruct((2 * T, rows), BF)),
        compiler_params=params(4),
        cost_estimate=cost(4_000_000, 200_000),
        name="prepare",
    )(ids, chances)
    sums = lax.all_to_all(sums, CTX, split_axis=0, concat_axis=0, tiled=True)

    own_residual = lax.dynamic_slice_in_dim(residual, ctx_index * 128, 128, 1)
    hidden, send = pl.pallas_call(
        dispatch_kernel,
        out_shape=(jax.ShapeDtypeStruct((T, 128), F32), jax.ShapeDtypeStruct((rows, 128), BF)),
        compiler_params=params(8),
        cost_estimate=cost(4_000_000, 500_000),
        name="dispatch",
    )(sums, own_residual, picker)
    arrived = lax.all_to_all(send.reshape(NG * NC, CAPE, 128), ALL, split_axis=0, concat_axis=0, tiled=True)

    results = pl.pallas_call(
        expert_kernel,
        in_specs=[vmem, vmem, vmem, vmem, hbm],
        out_shape=jax.ShapeDtypeStruct((rows, 128), BF),
        scratch_shapes=[pltpu.VMEM((rows, 128), F32), pltpu.VMEM((NG * CAPE, D), F32), pltpu.VMEM((FP, D), BF), pltpu.SemaphoreType.DMA(())],
        compiler_params=params(50),
        cost_estimate=cost(160_000_000, 5_300_000, 8192),
        name="experts",
    )(arrived.reshape(rows, 128), norm_gain.reshape(1, D), w_gate[0], w_up[0], w_down[0])
    returned = lax.all_to_all(results.reshape(NG * NC, CAPE, 128), ALL, split_axis=0, concat_axis=0, tiled=True)

    return pl.pallas_call(
        combine_kernel,
        out_shape=jax.ShapeDtypeStruct((T, 128), BF),
        compiler_params=params(8),
        cost_estimate=cost(8_000_000, 400_000),
        name="combine",
    )(returned.reshape(rows, 128), table, hidden)


def solution(mesh):
    fine = Mesh(mesh.devices.reshape(4, 2, 4, 8), ALL)
    placed = (
        P(GRP, None),
        P(GRP, CTX, None),
        P(GRP, CTX, None),
        P(GRP),
        P(ALL, None, None, None),
        P(CTX, GRP, None),
        P(CTX, GRP, None),
        P(CTX, None),
        P(GRP, None),
        P(),
        P(GRP, None),
        P(GRP, None),
        P(ALL, None, None),
        P(ALL, None, None),
        P(ALL, None, None),
    )
    return jax.shard_map(shards, mesh=fine, in_specs=placed, out_specs=P(GRP, CTX), check_vma=False)
```

```python
import functools

import jax
import jax.numpy as jnp
from jax import lax
from jax.experimental import pallas as pl
from jax.experimental.pallas import tpu as pltpu
from jax.sharding import Mesh, PartitionSpec as P

HEADS = 64
KV = 4
HPK = HEADS // KV
HW = 128
T = 16
D = 4096
NC = 32
NG = 8
CAPE = 4
FP = 192
TOK = 8
SLOTS = 16
EPS = 1e-06
NEG = -(2.0**100)
SCALE = HW**-0.5
BF = jnp.bfloat16
F32 = jnp.float32
GRP = ("y", "core")
CTX = ("x", "z")
ALL = GRP + CTX
NT = (((1,), (1,)), ((), ()))
STAT_ROWS = 8
EACH = 4
CHUNK = 2 * T + STAT_ROWS


def params(mib):
    return pltpu.CompilerParams(vmem_limit_bytes=mib * 2**20)


def cost(flops, moved, exps=0):
    return pl.CostEstimate(flops=flops, bytes_accessed=moved, transcendentals=exps)


def lists_kernel(key_ref, lists_ref):
    key = key_ref[...]
    lane = lax.broadcasted_iota(jnp.int32, (T, 128), 1)
    columns = [jnp.broadcast_to(key[:, j : j + 1], (T, 128)) - lane for j in range(key.shape[1])]
    for c in range(NC):
        hits = [column == c * 128 for column in columns]
        while len(hits) > 1:
            hits = [hits[i] | hits[i + 1] for i in range(0, len(hits), 2)]
        lists_ref[c] = jnp.where(hits[0], 1.0, 0.0).astype(BF)


def prepare_kernel(ids_ref, weights_ref, picker_ref, combine_ref):
    rows = NG * NC * CAPE
    one = (lax.broadcasted_iota(jnp.int32, (T, T), 1) == lax.broadcasted_iota(jnp.int32, (T, T), 0)).astype(F32)
    exact = dict(preferred_element_type=F32, precision=lax.Precision.HIGHEST)
    ids = lax.dot_general(one, ids_ref[...].astype(F32), NT, **exact)
    weights = lax.dot_general(one, weights_ref[...], NT, **exact)
    place = lax.broadcasted_iota(jnp.int32, (T, rows), 1)
    expert = (place // 16).astype(F32)
    slot = (place % CAPE).astype(F32)
    taken = jnp.zeros((T, rows), F32)
    coefficient = jnp.zeros((T, rows), F32)
    for j in range(ids_ref.shape[0]):
        hit = jnp.abs(jnp.broadcast_to(ids[:, j : j + 1], (T, rows)) - expert) < 0.5
        taken = taken + jnp.where(hit, 1.0, 0.0)
        coefficient = coefficient + jnp.where(hit, jnp.broadcast_to(weights[:, j : j + 1], (T, rows)), 0.0)
    before = (lax.broadcasted_iota(jnp.int32, (T, T), 1) < lax.broadcasted_iota(jnp.int32, (T, T), 0)).astype(F32)
    order = jnp.dot(before.astype(BF), taken.astype(BF), preferred_element_type=F32)
    hit = jnp.where((taken > 0.5) & (order == slot), 1.0, 0.0)
    picker_ref[...] = hit.astype(BF)
    table = hit * coefficient
    high = table.astype(BF)
    combine_ref[:T] = high
    combine_ref[T:] = (table - high.astype(F32)).astype(BF)


def resident_kernel(length_ref, start_ref, q_hbm, keys_hbm, values_hbm, out_ref, stats_ref, wide, q, k, v, sems):
    steps = k.shape[0] // EACH
    first = pltpu.make_async_copy(q_hbm, q, sems.at[2 * steps])
    first.start()

    def chunk(i):
        here = pl.ds(i * EACH, EACH)
        return (
            pltpu.make_async_copy(keys_hbm.at[here], k.at[here], sems.at[2 * i]),
            pltpu.make_async_copy(values_hbm.at[here], v.at[here], sems.at[2 * i + 1]),
        )

    for i in range(steps):
        for copy in chunk(i):
            copy.start()
    first.wait()
    for h in range(HEADS):
        head = q[:, h * HW : (h + 1) * HW]
        wide[h * T : (h + 1) * T, :] = head.astype(F32)

    position = lax.broadcasted_iota(jnp.int32, (HEADS, 128), 1) + start_ref[0]
    lane = lax.broadcasted_iota(jnp.int32, (HEADS, 128), 1)
    pairs = [(i, g) for i in range(EACH) for g in range(KV)]

    @pl.loop(0, steps)
    def _(step):
        for copy in chunk(step):
            copy.wait()
        base = step * EACH
        own = [wide[pl.ds(base + i, HEADS, stride=T), :].astype(BF) for i in range(EACH)]
        scores = [
            lax.dot_general(
                own[i][g * HPK : (g + 1) * HPK], k[base + i, :, g * HW : (g + 1) * HW], NT, preferred_element_type=F32
            )
            for i, g in pairs
        ]
        scores = jnp.concatenate(scores, axis=0).reshape(EACH, HEADS, 128)
        valid = [position < length_ref[base + i] for i in range(EACH)]
        scores = jnp.stack([jnp.where(valid[i], scores[i] * SCALE, NEG) for i in range(EACH)])
        peak = jnp.max(scores, axis=2, keepdims=True)
        chances = jnp.exp(scores - peak)
        chances = jnp.stack([jnp.where(valid[i], chances[i], 0.0) for i in range(EACH)])
        total = jnp.sum(chances, axis=2, keepdims=True)
        rounded = chances.astype(BF)
        out = [
            jnp.dot(
                rounded[i, g * HPK : (g + 1) * HPK],
                v[base + i, :, g * HW : (g + 1) * HW],
                preferred_element_type=F32,
            )
            for i, g in pairs
        ]
        for i in range(EACH):
            here = pl.ds(base + i, HEADS, stride=T)
            out_ref[here, :] = jnp.concatenate(out[i * KV : (i + 1) * KV], axis=0)
            stats_ref[here, :] = jnp.where(lane < 64, peak[i], total[i])


def recalled_kernel(half, lists_ref, q_ref, *refs):
    pages, given = refs[: NG // 2], refs[NG // 2 :]
    earlier, given = given[: 4 * half], given[4 * half :]
    rows = HPK * T
    tokens = len(pages) * SLOTS * TOK
    counts = jnp.sum(lists_ref[...].astype(F32), axis=0).astype(BF)
    spread = (
        lax.broadcasted_iota(jnp.int32, (128, tokens), 1) // TOK + half * (tokens // TOK)
        == lax.broadcasted_iota(jnp.int32, (128, tokens), 0)
    ).astype(F32)
    times = jnp.dot(counts, spread.astype(BF), preferred_element_type=F32)
    bias = jnp.where(times > 0.5, 0.0, NEG)[None]
    times = times[None]
    lanes = lax.broadcasted_iota(jnp.int32, (rows, 128), 1)
    kind = lanes % 4
    lane = lax.broadcasted_iota(jnp.int32, (HPK // 2, 8, 128), 2)
    for g in range(KV):
        own = slice(g * rows, (g + 1) * rows)
        columns = slice(g * HW, (g + 1) * HW)
        keys, values = [
            jnp.concatenate([ref[p, m, :, columns] for ref in pages for p in range(SLOTS)], axis=0) for m in range(2)
        ]
        heads = range(g * HPK, (g + 1) * HPK)
        queries = jnp.concatenate([q_ref[:, h * HW : (h + 1) * HW] for h in heads], axis=0)
        scores = lax.dot_general(queries, keys, NT, preferred_element_type=F32)
        scores = scores.reshape(HPK, T, tokens) * SCALE + bias
        peak = jnp.max(scores, axis=2, keepdims=True).reshape(rows, 1)
        peak = jnp.broadcast_to(peak, (rows, 128))
        joined = [(o[own, :], s[own, :]) for o, s in zip(earlier[::2], earlier[1::2], strict=True)]
        joined = [(o, jnp.broadcast_to(s[:, :1], (rows, 128)), s[:, 64:65]) for o, s in joined]
        for _, before, _ in joined:
            peak = jnp.maximum(peak, before)
        if half:
            peak_high = peak.astype(BF).astype(F32)
            peak_low = (peak - peak_high).astype(BF).astype(F32)
            base = peak_high + peak_low
        else:
            base = peak
        weights = jnp.exp(scores - base[:, :1].reshape(HPK, T, 1)) * times
        total = jnp.sum(weights, axis=2, keepdims=True).reshape(rows, 1)
        total = jnp.broadcast_to(total, (rows, 128))
        out = jnp.dot(weights.reshape(rows, tokens).astype(BF), values, preferred_element_type=F32)
        for o, before, t in joined:
            factor = jnp.exp(before - base)
            out = out + factor * o
            total = total + factor * jnp.broadcast_to(t, (rows, 128))
        if not half:
            given[0][own, :] = out
            given[1][own, :] = jnp.where(lanes < 64, base, total)
            continue
        total_high = total.astype(BF).astype(F32)
        stats = jnp.where(
            kind == 0, peak_high, jnp.where(kind == 1, peak_low, jnp.where(kind == 2, total_high, total - total_high))
        ).reshape(HPK // 2, 2, 2, 8, 128)
        here = slice(g * (HPK // 2), (g + 1) * (HPK // 2))
        given[0][here, : 2 * T, :] = out.reshape(HPK // 2, 2 * T, 128).astype(BF)
        stats = [jnp.where(lane < 4 + b, stats[:, 0, i], stats[:, 1, i]) for i, b in enumerate((0, 8))]
        given[0][here, 2 * T :, :] = jnp.where(lane < 8, *stats).astype(BF)


def project_kernel(parts_ref, weight_ref, send_ref):
    stats = parts_ref[:, 2 * T :, :].astype(F32)
    heads = []
    for i in range(2):
        high, low, total, rest = [
            jnp.concatenate([stats[:, :, 8 * b + 4 * i + q : 8 * b + 4 * i + q + 1] for b in range(2)], axis=1)
            for q in range(4)
        ]
        peak = high + low
        total = total + rest
        factor = jnp.exp(peak - jnp.max(peak, axis=0, keepdims=True))
        total = jnp.sum(factor * total, axis=0)
        out = jnp.sum(factor * parts_ref[:, i * T : (i + 1) * T, :].astype(F32), axis=0)
        heads.append((out / total).astype(BF))
    attention = jnp.concatenate(heads, axis=1)
    wide = 512
    for j in range(D // wide):
        block = jnp.dot(attention, weight_ref[:, j * wide : (j + 1) * wide], preferred_element_type=F32).astype(BF)
        for i in range(wide // 128):
            send_ref[j * (wide // 128) + i] = block[:, i * 128 : (i + 1) * 128]


def dispatch_kernel(start_ref, sums_ref, residual_ref, picker_ref, hidden_ref, send_ref):
    here = pl.ds(pl.multiple_of(start_ref[0], 128), 128)
    hidden = residual_ref[:, here].astype(F32) + jnp.sum(sums_ref[...].astype(F32), axis=0)
    hidden_ref[...] = hidden
    send_ref[...] = lax.dot_general(
        picker_ref[...], hidden.astype(BF), (((0,), (0,)), ((), ())), preferred_element_type=F32
    ).astype(BF)


def hidden_units_kernel(rows_ref, gain_ref, gate_ref, up_ref, act_ref, wide_ref, token_ref):
    wide_ref[...] = rows_ref[...].astype(F32)
    for c in range(NC):
        for s in range(CAPE):
            token_ref[s * NG : (s + 1) * NG, c * 128 : (c + 1) * 128] = wide_ref[pl.ds(c * CAPE + s, NG, stride=128), :]
    hidden = token_ref[...]
    normed = (hidden * lax.rsqrt(jnp.mean(hidden * hidden, axis=1, keepdims=True) + EPS) * gain_ref[...]).astype(BF)
    gate = lax.dot_general(normed, gate_ref[...], NT, preferred_element_type=F32)
    up = lax.dot_general(normed, up_ref[...], NT, preferred_element_type=F32)
    act_ref[...] = (gate / (1.0 + jnp.exp(-gate)) * up).astype(BF)


def down_kernel(act_ref, down_ref, send_ref, wide_ref):
    act = act_ref[...]
    wide = 512
    for j in range(D // wide):
        block = jnp.dot(act, down_ref[:, j * wide : (j + 1) * wide], preferred_element_type=F32)
        for i in range(wide // 128):
            for s in range(CAPE):
                wide_ref[pl.ds((j * (wide // 128) + i) * CAPE + s, NG, stride=128), :] = block[
                    s * NG : (s + 1) * NG, i * 128 : (i + 1) * 128
                ]
    send_ref[...] = wide_ref[...].astype(BF)


def combine_kernel(rows_ref, table_ref, hidden_ref, out_ref):
    both = jnp.dot(table_ref[...], rows_ref[...], preferred_element_type=F32)
    out_ref[...] = (hidden_ref[...] + both[:T] + both[T:]).astype(BF)


def shards(
    queries,
    resident_key_cache,
    resident_value_cache,
    res_len,
    visual_page_pool,
    recall_holder,
    recall_slot,
    o_weight,
    residual,
    norm_gain,
    expert_ids,
    expert_weights,
    w_gate,
    w_up,
    w_down,
):
    ctx_index = lax.axis_index(CTX)
    rows = NG * NC * CAPE
    start = (ctx_index * 128).reshape(1).astype(jnp.int32)

    smem = pl.BlockSpec(memory_space=pltpu.SMEM)
    vmem = pl.BlockSpec(memory_space=pltpu.VMEM)
    hbm = pl.BlockSpec(memory_space=pltpu.HBM)
    pages = [visual_page_pool]
    for k in range(1, 4):
        pages.append(lax.ppermute(visual_page_pool, "y", [(i, (i + k) % 4) for i in range(4)]))
    pages += [lax.ppermute(part, "core", [(0, 1), (1, 0)]) for part in pages]

    holder = recall_holder[0]
    group = holder // NC
    back = (lax.axis_index("y") + 4 - group // 2) % 4
    near = jnp.where(group % 2 == lax.axis_index("core"), back, back + 4)
    key = (holder % NC) * 128 + near * SLOTS + recall_slot[0]
    lists = pl.pallas_call(
        lists_kernel,
        out_shape=jax.ShapeDtypeStruct((NC, T, 128), BF),
        compiler_params=params(4),
        cost_estimate=cost(4_000_000, 140_000),
        name="lists",
    )(key)
    lists = lax.all_to_all(lists, CTX, split_axis=0, concat_axis=0, tiled=True)

    wide = jax.ShapeDtypeStruct((HEADS * T, 128), F32)
    out, stats = pl.pallas_call(
        resident_kernel,
        in_specs=[smem, smem, hbm, hbm, hbm],
        out_shape=(wide, wide),
        scratch_shapes=[
            pltpu.VMEM((HEADS * T, HW), F32),
            pltpu.VMEM((T, HEADS * HW), BF),
            pltpu.VMEM((T, 128, KV * HW), BF),
            pltpu.VMEM((T, 128, KV * HW), BF),
            pltpu.SemaphoreType.DMA((2 * T // EACH + 1,)),
        ],
        compiler_params=params(51),
        cost_estimate=cost(70_000_000, 6_000_000, 131_072),
        name="resident",
    )(res_len, start, queries, resident_key_cache, resident_value_cache)

    own = pl.pallas_call(
        functools.partial(recalled_kernel, 0),
        out_shape=(wide, wide),
        compiler_params=params(16),
        cost_estimate=cost(270_000_000, 4_000_000, 524_288),
        name="recalled_own",
    )(lists, queries, *pages[:4])
    parts = pl.pallas_call(
        functools.partial(recalled_kernel, 1),
        out_shape=jax.ShapeDtypeStruct((NC, CHUNK, 128), BF),
        compiler_params=params(16),
        cost_estimate=cost(270_000_000, 4_000_000, 524_288),
        name="recalled_other",
    )(lists, queries, *pages[4:], *own, out, stats)
    parts = lax.all_to_all(parts, CTX, split_axis=0, concat_axis=0, tiled=True)

    sums = pl.pallas_call(
        project_kernel,
        out_shape=jax.ShapeDtypeStruct((NC, T, 128), BF),
        compiler_params=params(8),
        cost_estimate=cost(40_000_000, 2_700_000, 2048),
        name="project",
    )(parts, o_weight)
    ids, chances, _ = lax.optimization_barrier((expert_ids.T, expert_weights.T, sums))
    picker, table = pl.pallas_call(
        prepare_kernel,
        out_shape=(jax.ShapeDtypeStruct((T, rows), BF), jax.ShapeDtypeStruct((2 * T, rows), BF)),
        compiler_params=params(4),
        cost_estimate=cost(4_000_000, 200_000),
        name="prepare",
    )(ids, chances)
    sums = lax.all_to_all(sums, CTX, split_axis=0, concat_axis=0, tiled=True)

    hidden, send = pl.pallas_call(
        dispatch_kernel,
        in_specs=[smem, vmem, vmem, vmem],
        out_shape=(jax.ShapeDtypeStruct((T, 128), F32), jax.ShapeDtypeStruct((rows, 128), BF)),
        compiler_params=params(8),
        cost_estimate=cost(4_000_000, 500_000),
        name="dispatch",
    )(start, sums, residual, picker)
    arrived = lax.all_to_all(send.reshape(NG * NC, CAPE, 128), ALL, split_axis=0, concat_axis=0, tiled=True)

    act = pl.pallas_call(
        hidden_units_kernel,
        out_shape=jax.ShapeDtypeStruct((NG * CAPE, FP), BF),
        scratch_shapes=[pltpu.VMEM((rows, 128), F32), pltpu.VMEM((NG * CAPE, D), F32)],
        compiler_params=params(8),
        cost_estimate=cost(100_000_000, 3_500_000, 8192),
        name="hidden_units",
    )(arrived.reshape(rows, 128), norm_gain.reshape(1, D), w_gate[0], w_up[0])
    results = pl.pallas_call(
        down_kernel,
        out_shape=jax.ShapeDtypeStruct((rows, 128), BF),
        scratch_shapes=[pltpu.VMEM((rows, 128), F32)],
        compiler_params=params(8),
        cost_estimate=cost(50_000_000, 1_900_000),
        name="down",
    )(act, w_down[0])
    returned = lax.all_to_all(results.reshape(NG * NC, CAPE, 128), ALL, split_axis=0, concat_axis=0, tiled=True)

    return pl.pallas_call(
        combine_kernel,
        out_shape=jax.ShapeDtypeStruct((T, 128), BF),
        compiler_params=params(8),
        cost_estimate=cost(8_000_000, 400_000),
        name="combine",
    )(returned.reshape(rows, 128), table, hidden)


def solution(mesh):
    fine = Mesh(mesh.devices.reshape(4, 2, 4, 8), ALL)
    placed = (
        P(GRP, None),
        P(GRP, CTX, None),
        P(GRP, CTX, None),
        P(GRP),
        P(ALL, None, None, None),
        P(CTX, GRP, None),
        P(CTX, GRP, None),
        P(CTX, None),
        P(GRP, None),
        P(),
        P(GRP, None),
        P(GRP, None),
        P(ALL, None, None),
        P(ALL, None, None),
        P(ALL, None, None),
    )
    return jax.shard_map(shards, mesh=fine, in_specs=placed, out_specs=P(GRP, CTX), check_vma=False)
```

```python
import functools

import jax
import jax.numpy as jnp
from jax import lax
from jax.experimental import pallas as pl
from jax.experimental.pallas import tpu as pltpu
from jax.sharding import Mesh, PartitionSpec as P

HEADS = 64
KV = 4
HPK = HEADS // KV
HW = 128
T = 16
D = 4096
NC = 32
NG = 8
CAPE = 4
FP = 192
TOK = 8
SLOTS = 16
EPS = 1e-06
NEG = -(2.0**100)
SCALE = HW**-0.5
BF = jnp.bfloat16
F32 = jnp.float32
GRP = ("y", "core")
CTX = ("x", "z")
ALL = GRP + CTX
NT = (((1,), (1,)), ((), ()))
STAT_ROWS = 8
EACH = 4
CHUNK = 2 * T + STAT_ROWS


def params(mib):
    return pltpu.CompilerParams(vmem_limit_bytes=mib * 2**20)


def cost(flops, moved, exps=0):
    return pl.CostEstimate(flops=flops, bytes_accessed=moved, transcendentals=exps)


def lists_kernel(key_ref, lists_ref, lengths_ref):
    key = key_ref[:, :SLOTS]
    lengths_ref[...] = jnp.broadcast_to(key_ref[:, SLOTS:], (T, 128))
    lane = lax.broadcasted_iota(jnp.int32, (T, 128), 1)
    columns = [jnp.broadcast_to(key[:, j : j + 1], (T, 128)) - lane for j in range(key.shape[1])]
    for c in range(NC):
        hits = [column == c * 128 for column in columns]
        while len(hits) > 1:
            hits = [hits[i] | hits[i + 1] for i in range(0, len(hits), 2)]
        lists_ref[c] = jnp.where(hits[0], 1.0, 0.0).astype(BF)


def prepare(ids_ref, weights_ref, picker_ref, combine_ref):
    rows = NG * NC * CAPE
    one = (lax.broadcasted_iota(jnp.int32, (T, T), 1) == lax.broadcasted_iota(jnp.int32, (T, T), 0)).astype(F32)
    exact = dict(preferred_element_type=F32, precision=lax.Precision.HIGHEST)
    ids = lax.dot_general(one, ids_ref[...].astype(F32), NT, **exact)
    weights = lax.dot_general(one, weights_ref[...], NT, **exact)
    place = lax.broadcasted_iota(jnp.int32, (T, rows), 1)
    expert = (place // 16).astype(F32)
    slot = (place % CAPE).astype(F32)
    taken = jnp.zeros((T, rows), F32)
    coefficient = jnp.zeros((T, rows), F32)
    for j in range(ids_ref.shape[0]):
        hit = jnp.abs(jnp.broadcast_to(ids[:, j : j + 1], (T, rows)) - expert) < 0.5
        taken = taken + jnp.where(hit, 1.0, 0.0)
        coefficient = coefficient + jnp.where(hit, jnp.broadcast_to(weights[:, j : j + 1], (T, rows)), 0.0)
    before = (lax.broadcasted_iota(jnp.int32, (T, T), 1) < lax.broadcasted_iota(jnp.int32, (T, T), 0)).astype(F32)
    order = jnp.dot(before.astype(BF), taken.astype(BF), preferred_element_type=F32)
    hit = jnp.where((taken > 0.5) & (order == slot), 1.0, 0.0)
    picker_ref[...] = hit.astype(BF)
    table = hit * coefficient
    high = table.astype(BF)
    combine_ref[:T] = high
    combine_ref[T:] = (table - high.astype(F32)).astype(BF)


def resident_kernel(length_ref, start_ref, q_hbm, keys_hbm, values_hbm, out_ref, stats_ref, wide, q, k, v, sems):
    steps = k.shape[0] // EACH
    first = pltpu.make_async_copy(q_hbm, q, sems.at[2 * steps])
    first.start()

    def chunk(i):
        here = pl.ds(i * EACH, EACH)
        return (
            pltpu.make_async_copy(keys_hbm.at[here], k.at[here], sems.at[2 * i]),
            pltpu.make_async_copy(values_hbm.at[here], v.at[here], sems.at[2 * i + 1]),
        )

    for i in range(steps):
        for copy in chunk(i):
            copy.start()
    first.wait()
    for h in range(HEADS):
        head = q[:, h * HW : (h + 1) * HW]
        wide[h * T : (h + 1) * T, :] = head.astype(F32)

    position = lax.broadcasted_iota(jnp.int32, (HEADS, 128), 1) + start_ref[0]
    lane = lax.broadcasted_iota(jnp.int32, (HEADS, 128), 1)
    pairs = [(i, g) for i in range(EACH) for g in range(KV)]

    @pl.loop(0, steps)
    def _(step):
        for copy in chunk(step):
            copy.wait()
        base = step * EACH
        own = [wide[pl.ds(base + i, HEADS, stride=T), :].astype(BF) for i in range(EACH)]
        scores = [
            lax.dot_general(
                own[i][g * HPK : (g + 1) * HPK], k[base + i, :, g * HW : (g + 1) * HW], NT, preferred_element_type=F32
            )
            for i, g in pairs
        ]
        scores = jnp.concatenate(scores, axis=0).reshape(EACH, HEADS, 128)
        valid = [position < length_ref[pl.ds(base + i, 1), :] for i in range(EACH)]
        scores = jnp.stack([jnp.where(valid[i], scores[i] * SCALE, NEG) for i in range(EACH)])
        peak = jnp.max(scores, axis=2, keepdims=True)
        chances = jnp.exp(scores - peak)
        chances = jnp.stack([jnp.where(valid[i], chances[i], 0.0) for i in range(EACH)])
        total = jnp.sum(chances, axis=2, keepdims=True)
        rounded = chances.astype(BF)
        out = [
            jnp.dot(
                rounded[i, g * HPK : (g + 1) * HPK],
                v[base + i, :, g * HW : (g + 1) * HW],
                preferred_element_type=F32,
            )
            for i, g in pairs
        ]
        for i in range(EACH):
            here = pl.ds(base + i, HEADS, stride=T)
            out_ref[here, :] = jnp.concatenate(out[i * KV : (i + 1) * KV], axis=0)
            stats_ref[here, :] = jnp.where(lane < 64, peak[i], total[i])


def recalled_kernel(half, lists_ref, q_ref, *refs):
    pages, given = refs[: NG // 2], refs[NG // 2 :]
    earlier, given = given[: 4 * half], given[4 * half :]
    rows = HPK * T
    tokens = len(pages) * SLOTS * TOK
    counts = jnp.sum(lists_ref[...].astype(F32), axis=0).astype(BF)
    spread = (
        lax.broadcasted_iota(jnp.int32, (128, tokens), 1) // TOK + half * (tokens // TOK)
        == lax.broadcasted_iota(jnp.int32, (128, tokens), 0)
    ).astype(F32)
    times = jnp.dot(counts, spread.astype(BF), preferred_element_type=F32)
    bias = jnp.where(times > 0.5, 0.0, NEG)[None]
    times = times[None]
    lanes = lax.broadcasted_iota(jnp.int32, (rows, 128), 1)
    kind = lanes % 4
    lane = lax.broadcasted_iota(jnp.int32, (HPK // 2, 8, 128), 2)
    for g in range(KV):
        own = slice(g * rows, (g + 1) * rows)
        columns = slice(g * HW, (g + 1) * HW)
        keys, values = [
            jnp.concatenate([ref[p, m, :, columns] for ref in pages for p in range(SLOTS)], axis=0) for m in range(2)
        ]
        heads = range(g * HPK, (g + 1) * HPK)
        queries = jnp.concatenate([q_ref[:, h * HW : (h + 1) * HW] for h in heads], axis=0)
        scores = lax.dot_general(queries, keys, NT, preferred_element_type=F32)
        scores = scores.reshape(HPK, T, tokens) * SCALE + bias
        peak = jnp.max(scores, axis=2, keepdims=True).reshape(rows, 1)
        peak = jnp.broadcast_to(peak, (rows, 128))
        joined = [(o[own, :], s[own, :]) for o, s in zip(earlier[::2], earlier[1::2], strict=True)]
        joined = [(o, jnp.broadcast_to(s[:, :1], (rows, 128)), s[:, 64:65]) for o, s in joined]
        for _, before, _ in joined:
            peak = jnp.maximum(peak, before)
        if half:
            peak_high = peak.astype(BF).astype(F32)
            peak_low = (peak - peak_high).astype(BF).astype(F32)
            base = peak_high + peak_low
        else:
            base = peak
        weights = jnp.exp(scores - base[:, :1].reshape(HPK, T, 1)) * times
        total = jnp.sum(weights, axis=2, keepdims=True).reshape(rows, 1)
        total = jnp.broadcast_to(total, (rows, 128))
        out = jnp.dot(weights.reshape(rows, tokens).astype(BF), values, preferred_element_type=F32)
        for o, before, t in joined:
            factor = jnp.exp(before - base)
            out = out + factor * o
            total = total + factor * jnp.broadcast_to(t, (rows, 128))
        if not half:
            given[0][own, :] = out
            given[1][own, :] = jnp.where(lanes < 64, base, total)
            continue
        total_high = total.astype(BF).astype(F32)
        stats = jnp.where(
            kind == 0, peak_high, jnp.where(kind == 1, peak_low, jnp.where(kind == 2, total_high, total - total_high))
        ).reshape(HPK // 2, 2, 2, 8, 128)
        here = slice(g * (HPK // 2), (g + 1) * (HPK // 2))
        given[0][here, : 2 * T, :] = out.reshape(HPK // 2, 2 * T, 128).astype(BF)
        stats = [jnp.where(lane < 4 + b, stats[:, 0, i], stats[:, 1, i]) for i, b in enumerate((0, 8))]
        given[0][here, 2 * T :, :] = jnp.where(lane < 8, *stats).astype(BF)


def project_kernel(ids_ref, chances_ref, parts_ref, weight_ref, send_ref, picker_ref, combine_ref):
    prepare(ids_ref, chances_ref, picker_ref, combine_ref)
    stats = parts_ref[:, 2 * T :, :].astype(F32)
    heads = []
    for i in range(2):
        high, low, total, rest = [
            jnp.concatenate([stats[:, :, 8 * b + 4 * i + q : 8 * b + 4 * i + q + 1] for b in range(2)], axis=1)
            for q in range(4)
        ]
        peak = high + low
        total = total + rest
        factor = jnp.exp(peak - jnp.max(peak, axis=0, keepdims=True))
        total = jnp.sum(factor * total, axis=0)
        out = jnp.sum(factor * parts_ref[:, i * T : (i + 1) * T, :].astype(F32), axis=0)
        heads.append((out / total).astype(BF))
    attention = jnp.concatenate(heads, axis=1)
    wide = 512
    for j in range(D // wide):
        block = jnp.dot(attention, weight_ref[:, j * wide : (j + 1) * wide], preferred_element_type=F32).astype(BF)
        for i in range(wide // 128):
            send_ref[j * (wide // 128) + i] = block[:, i * 128 : (i + 1) * 128]


def dispatch_kernel(start_ref, sums_ref, residual_ref, picker_ref, hidden_ref, send_ref):
    here = pl.ds(pl.multiple_of(start_ref[0], 128), 128)
    hidden = residual_ref[:, here].astype(F32) + jnp.sum(sums_ref[...].astype(F32), axis=0)
    hidden_ref[...] = hidden
    send_ref[...] = lax.dot_general(
        picker_ref[...], hidden.astype(BF), (((0,), (0,)), ((), ())), preferred_element_type=F32
    ).astype(BF)


def hidden_units_kernel(rows_ref, gain_ref, gate_ref, up_ref, act_ref, wide_ref, token_ref):
    wide_ref[...] = rows_ref[...].astype(F32)
    for c in range(NC):
        for s in range(CAPE):
            token_ref[s * NG : (s + 1) * NG, c * 128 : (c + 1) * 128] = wide_ref[pl.ds(c * CAPE + s, NG, stride=128), :]
    hidden = token_ref[...]
    normed = (hidden * lax.rsqrt(jnp.mean(hidden * hidden, axis=1, keepdims=True) + EPS) * gain_ref[...]).astype(BF)
    gate = lax.dot_general(normed, gate_ref[...], NT, preferred_element_type=F32)
    up = lax.dot_general(normed, up_ref[...], NT, preferred_element_type=F32)
    act_ref[...] = (gate / (1.0 + jnp.exp(-gate)) * up).astype(BF)


def down_kernel(act_ref, down_ref, send_ref, wide_ref):
    act = act_ref[...]
    wide = 512
    for j in range(D // wide):
        block = jnp.dot(act, down_ref[:, j * wide : (j + 1) * wide], preferred_element_type=F32)
        for i in range(wide // 128):
            for s in range(CAPE):
                wide_ref[pl.ds((j * (wide // 128) + i) * CAPE + s, NG, stride=128), :] = block[
                    s * NG : (s + 1) * NG, i * 128 : (i + 1) * 128
                ]
    send_ref[...] = wide_ref[...].astype(BF)


def combine_kernel(rows_ref, table_ref, hidden_ref, out_ref):
    both = jnp.dot(table_ref[...], rows_ref[...], preferred_element_type=F32)
    out_ref[...] = (hidden_ref[...] + both[:T] + both[T:]).astype(BF)


def shards(
    queries,
    resident_key_cache,
    resident_value_cache,
    res_len,
    visual_page_pool,
    recall_holder,
    recall_slot,
    o_weight,
    residual,
    norm_gain,
    expert_ids,
    expert_weights,
    w_gate,
    w_up,
    w_down,
):
    ctx_index = lax.axis_index(CTX)
    rows = NG * NC * CAPE
    start = (ctx_index * 128).reshape(1).astype(jnp.int32)

    smem = pl.BlockSpec(memory_space=pltpu.SMEM)
    vmem = pl.BlockSpec(memory_space=pltpu.VMEM)
    hbm = pl.BlockSpec(memory_space=pltpu.HBM)
    pages = [visual_page_pool]
    for k in range(1, 4):
        pages.append(lax.ppermute(visual_page_pool, "y", [(i, (i + k) % 4) for i in range(4)]))
    pages += [lax.ppermute(part, "core", [(0, 1), (1, 0)]) for part in pages]

    pad = ((0, 0), (0, 1))
    holder, slot = jnp.pad(recall_holder[0], pad), jnp.pad(recall_slot[0], pad)
    group = holder // NC
    back = (lax.axis_index("y") + 4 - group // 2) % 4
    near = jnp.where(group % 2 == lax.axis_index("core"), back, back + 4)
    key = (holder % NC) * 128 + near * SLOTS + slot
    column = lax.broadcasted_iota(jnp.int32, key.shape, 1)
    key = jnp.where(column < SLOTS, key, res_len[:, None])
    lists, lengths = pl.pallas_call(
        lists_kernel,
        out_shape=(jax.ShapeDtypeStruct((NC, T, 128), BF), jax.ShapeDtypeStruct((T, 128), jnp.int32)),
        compiler_params=params(4),
        cost_estimate=cost(4_000_000, 140_000),
        name="lists",
    )(key)
    lists = lax.all_to_all(lists, CTX, split_axis=0, concat_axis=0, tiled=True)

    wide = jax.ShapeDtypeStruct((HEADS * T, 128), F32)
    out, stats = pl.pallas_call(
        resident_kernel,
        in_specs=[vmem, smem, hbm, hbm, hbm],
        out_shape=(wide, wide),
        scratch_shapes=[
            pltpu.VMEM((HEADS * T, HW), F32),
            pltpu.VMEM((T, HEADS * HW), BF),
            pltpu.VMEM((T, 128, KV * HW), BF),
            pltpu.VMEM((T, 128, KV * HW), BF),
            pltpu.SemaphoreType.DMA((2 * T // EACH + 1,)),
        ],
        compiler_params=params(51),
        cost_estimate=cost(70_000_000, 6_000_000, 131_072),
        name="resident",
    )(lengths, start, queries, resident_key_cache, resident_value_cache)

    own = pl.pallas_call(
        functools.partial(recalled_kernel, 0),
        out_shape=(wide, wide),
        compiler_params=params(16),
        cost_estimate=cost(270_000_000, 4_000_000, 524_288),
        name="recalled_own",
    )(lists, queries, *pages[:4])
    parts = pl.pallas_call(
        functools.partial(recalled_kernel, 1),
        out_shape=jax.ShapeDtypeStruct((NC, CHUNK, 128), BF),
        compiler_params=params(16),
        cost_estimate=cost(270_000_000, 4_000_000, 524_288),
        name="recalled_other",
    )(lists, queries, *pages[4:], *own, out, stats)
    parts = lax.all_to_all(parts, CTX, split_axis=0, concat_axis=0, tiled=True)

    sums, picker, table = pl.pallas_call(
        project_kernel,
        out_shape=(
            jax.ShapeDtypeStruct((NC, T, 128), BF),
            jax.ShapeDtypeStruct((T, rows), BF),
            jax.ShapeDtypeStruct((2 * T, rows), BF),
        ),
        compiler_params=params(8),
        cost_estimate=cost(44_000_000, 2_900_000, 2048),
        name="project",
    )(expert_ids.T, expert_weights.T, parts, o_weight)
    sums = lax.all_to_all(sums, CTX, split_axis=0, concat_axis=0, tiled=True)

    hidden, send = pl.pallas_call(
        dispatch_kernel,
        in_specs=[smem, vmem, vmem, vmem],
        out_shape=(jax.ShapeDtypeStruct((T, 128), F32), jax.ShapeDtypeStruct((rows, 128), BF)),
        compiler_params=params(8),
        cost_estimate=cost(4_000_000, 500_000),
        name="dispatch",
    )(start, sums, residual, picker)
    arrived = lax.all_to_all(send.reshape(NG * NC, CAPE, 128), ALL, split_axis=0, concat_axis=0, tiled=True)

    act = pl.pallas_call(
        hidden_units_kernel,
        out_shape=jax.ShapeDtypeStruct((NG * CAPE, FP), BF),
        scratch_shapes=[pltpu.VMEM((rows, 128), F32), pltpu.VMEM((NG * CAPE, D), F32)],
        compiler_params=params(8),
        cost_estimate=cost(100_000_000, 3_500_000, 8192),
        name="hidden_units",
    )(arrived.reshape(rows, 128), norm_gain.reshape(1, D), w_gate[0], w_up[0])
    results = pl.pallas_call(
        down_kernel,
        out_shape=jax.ShapeDtypeStruct((rows, 128), BF),
        scratch_shapes=[pltpu.VMEM((rows, 128), F32)],
        compiler_params=params(8),
        cost_estimate=cost(50_000_000, 1_900_000),
        name="down",
    )(act, w_down[0])
    returned = lax.all_to_all(results.reshape(NG * NC, CAPE, 128), ALL, split_axis=0, concat_axis=0, tiled=True)

    return pl.pallas_call(
        combine_kernel,
        out_shape=jax.ShapeDtypeStruct((T, 128), BF),
        compiler_params=params(8),
        cost_estimate=cost(8_000_000, 400_000),
        name="combine",
    )(returned.reshape(rows, 128), table, hidden)


def solution(mesh):
    fine = Mesh(mesh.devices.reshape(4, 2, 4, 8), ALL)
    placed = (
        P(GRP, None),
        P(GRP, CTX, None),
        P(GRP, CTX, None),
        P(GRP),
        P(ALL, None, None, None),
        P(CTX, GRP, None),
        P(CTX, GRP, None),
        P(CTX, None),
        P(GRP, None),
        P(),
        P(GRP, None),
        P(GRP, None),
        P(ALL, None, None),
        P(ALL, None, None),
        P(ALL, None, None),
    )
    return jax.shard_map(shards, mesh=fine, in_specs=placed, out_specs=P(GRP, CTX), check_vma=False)
```

```python
import functools

import jax
import jax.numpy as jnp
from jax import lax
from jax.experimental import pallas as pl
from jax.experimental.pallas import tpu as pltpu
from jax.sharding import Mesh, PartitionSpec as P

HEADS = 64
KV = 4
HPK = HEADS // KV
HW = 128
T = 16
D = 4096
NC = 32
NG = 8
CAPE = 4
FP = 192
TOK = 8
SLOTS = 16
EPS = 1e-06
NEG = -(2.0**100)
SCALE = HW**-0.5
BF = jnp.bfloat16
F32 = jnp.float32
GRP = ("y", "core")
CTX = ("x", "z")
ALL = GRP + CTX
NT = (((1,), (1,)), ((), ()))
STAT_ROWS = 8
EACH = 8
FETCH = 4
CHUNK = 2 * T + STAT_ROWS


def params(mib):
    return pltpu.CompilerParams(vmem_limit_bytes=mib * 2**20)


def cost(flops, moved, exps=0):
    return pl.CostEstimate(flops=flops, bytes_accessed=moved, transcendentals=exps)


def lists_kernel(key_ref, lists_ref, lengths_ref):
    key = key_ref[:, :SLOTS]
    lengths_ref[...] = jnp.broadcast_to(key_ref[:, SLOTS:], (T, 128))
    lane = lax.broadcasted_iota(jnp.int32, (T, 128), 1)
    columns = [jnp.broadcast_to(key[:, j : j + 1], (T, 128)) - lane for j in range(key.shape[1])]
    for c in range(NC):
        hits = [column == c * 128 for column in columns]
        while len(hits) > 1:
            hits = [hits[i] | hits[i + 1] for i in range(0, len(hits), 2)]
        lists_ref[c] = jnp.where(hits[0], 1.0, 0.0).astype(BF)


def prepare(ids_ref, weights_ref, picker_ref, combine_ref):
    rows = NG * NC * CAPE
    one = (lax.broadcasted_iota(jnp.int32, (T, T), 1) == lax.broadcasted_iota(jnp.int32, (T, T), 0)).astype(F32)
    exact = dict(preferred_element_type=F32, precision=lax.Precision.HIGHEST)
    ids = lax.dot_general(one, ids_ref[...].astype(F32), NT, **exact)
    weights = lax.dot_general(one, weights_ref[...], NT, **exact)
    place = lax.broadcasted_iota(jnp.int32, (T, rows), 1)
    expert = (place // 16).astype(F32)
    slot = (place % CAPE).astype(F32)
    taken = jnp.zeros((T, rows), F32)
    coefficient = jnp.zeros((T, rows), F32)
    for j in range(ids_ref.shape[0]):
        hit = jnp.abs(jnp.broadcast_to(ids[:, j : j + 1], (T, rows)) - expert) < 0.5
        taken = taken + jnp.where(hit, 1.0, 0.0)
        coefficient = coefficient + jnp.where(hit, jnp.broadcast_to(weights[:, j : j + 1], (T, rows)), 0.0)
    before = (lax.broadcasted_iota(jnp.int32, (T, T), 1) < lax.broadcasted_iota(jnp.int32, (T, T), 0)).astype(F32)
    order = jnp.dot(before.astype(BF), taken.astype(BF), preferred_element_type=F32)
    hit = jnp.where((taken > 0.5) & (order == slot), 1.0, 0.0)
    picker_ref[...] = hit.astype(BF)
    table = hit * coefficient
    high = table.astype(BF)
    combine_ref[:T] = high
    combine_ref[T:] = (table - high.astype(F32)).astype(BF)


def resident_kernel(length_ref, start_ref, q_hbm, keys_hbm, values_hbm, out_ref, stats_ref, wide, q, k, v, sems):
    steps, fetches = k.shape[0] // EACH, k.shape[0] // FETCH
    first = pltpu.make_async_copy(q_hbm, q, sems.at[2 * fetches])
    first.start()

    def chunk(i):
        here = pl.ds(i * FETCH, FETCH)
        return (
            pltpu.make_async_copy(keys_hbm.at[here], k.at[here], sems.at[2 * i]),
            pltpu.make_async_copy(values_hbm.at[here], v.at[here], sems.at[2 * i + 1]),
        )

    for i in range(fetches):
        for copy in chunk(i):
            copy.start()
    first.wait()
    for h in range(HEADS):
        head = q[:, h * HW : (h + 1) * HW]
        wide[h * T : (h + 1) * T, :] = head.astype(F32)

    position = lax.broadcasted_iota(jnp.int32, (HEADS, 128), 1) + start_ref[0]
    lane = lax.broadcasted_iota(jnp.int32, (HEADS, 128), 1)
    pairs = [(i, g) for i in range(EACH) for g in range(KV)]

    @pl.loop(0, steps)
    def _(step):
        for i in range(EACH // FETCH):
            for copy in chunk(step * (EACH // FETCH) + i):
                copy.wait()
        base = step * EACH
        own = [wide[pl.ds(base + i, HEADS, stride=T), :].astype(BF) for i in range(EACH)]
        scores = [
            lax.dot_general(
                own[i][g * HPK : (g + 1) * HPK], k[base + i, :, g * HW : (g + 1) * HW], NT, preferred_element_type=F32
            )
            for i, g in pairs
        ]
        scores = jnp.concatenate(scores, axis=0).reshape(EACH, HEADS, 128)
        valid = [position < length_ref[pl.ds(base + i, 1), :] for i in range(EACH)]
        scores = jnp.stack([jnp.where(valid[i], scores[i] * SCALE, NEG) for i in range(EACH)])
        peak = jnp.max(scores, axis=2, keepdims=True)
        chances = jnp.exp(scores - peak)
        chances = jnp.stack([jnp.where(valid[i], chances[i], 0.0) for i in range(EACH)])
        total = jnp.sum(chances, axis=2, keepdims=True)
        rounded = chances.astype(BF)
        out = [
            jnp.dot(
                rounded[i, g * HPK : (g + 1) * HPK],
                v[base + i, :, g * HW : (g + 1) * HW],
                preferred_element_type=F32,
            )
            for i, g in pairs
        ]
        for i in range(EACH):
            here = pl.ds(base + i, HEADS, stride=T)
            out_ref[here, :] = jnp.concatenate(out[i * KV : (i + 1) * KV], axis=0)
            stats_ref[here, :] = jnp.where(lane < 64, peak[i], total[i])


def recalled_kernel(half, lists_ref, q_ref, *refs):
    pages, given = refs[: NG // 2], refs[NG // 2 :]
    earlier, given = given[: 4 * half], given[4 * half :]
    rows = HPK * T
    tokens = len(pages) * SLOTS * TOK
    counts = jnp.sum(lists_ref[...].astype(F32), axis=0).astype(BF)
    spread = (
        lax.broadcasted_iota(jnp.int32, (128, tokens), 1) // TOK + half * (tokens // TOK)
        == lax.broadcasted_iota(jnp.int32, (128, tokens), 0)
    ).astype(F32)
    times = jnp.dot(counts, spread.astype(BF), preferred_element_type=F32)
    bias = jnp.where(times > 0.5, 0.0, NEG)[None]
    times = times[None]
    lanes = lax.broadcasted_iota(jnp.int32, (rows, 128), 1)
    kind = lanes % 4
    lane = lax.broadcasted_iota(jnp.int32, (HPK // 2, 8, 128), 2)
    for g in range(KV):
        own = slice(g * rows, (g + 1) * rows)
        columns = slice(g * HW, (g + 1) * HW)
        keys, values = [
            jnp.concatenate([ref[p, m, :, columns] for ref in pages for p in range(SLOTS)], axis=0) for m in range(2)
        ]
        heads = range(g * HPK, (g + 1) * HPK)
        queries = jnp.concatenate([q_ref[:, h * HW : (h + 1) * HW] for h in heads], axis=0)
        scores = lax.dot_general(queries, keys, NT, preferred_element_type=F32)
        scores = scores.reshape(HPK, T, tokens) * SCALE + bias
        peak = jnp.max(scores, axis=2, keepdims=True).reshape(rows, 1)
        peak = jnp.broadcast_to(peak, (rows, 128))
        joined = [(o[own, :], s[own, :]) for o, s in zip(earlier[::2], earlier[1::2], strict=True)]
        joined = [(o, jnp.broadcast_to(s[:, :1], (rows, 128)), s[:, 64:65]) for o, s in joined]
        for _, before, _ in joined:
            peak = jnp.maximum(peak, before)
        if half:
            peak_high = peak.astype(BF).astype(F32)
            peak_low = (peak - peak_high).astype(BF).astype(F32)
            base = peak_high + peak_low
        else:
            base = peak
        weights = jnp.exp(scores - base[:, :1].reshape(HPK, T, 1)) * times
        total = jnp.sum(weights, axis=2, keepdims=True).reshape(rows, 1)
        total = jnp.broadcast_to(total, (rows, 128))
        out = jnp.dot(weights.reshape(rows, tokens).astype(BF), values, preferred_element_type=F32)
        for o, before, t in joined:
            factor = jnp.exp(before - base)
            out = out + factor * o
            total = total + factor * jnp.broadcast_to(t, (rows, 128))
        if not half:
            given[0][own, :] = out
            given[1][own, :] = jnp.where(lanes < 64, base, total)
            continue
        total_high = total.astype(BF).astype(F32)
        stats = jnp.where(
            kind == 0, peak_high, jnp.where(kind == 1, peak_low, jnp.where(kind == 2, total_high, total - total_high))
        ).reshape(HPK // 2, 2, 2, 8, 128)
        here = slice(g * (HPK // 2), (g + 1) * (HPK // 2))
        given[0][here, : 2 * T, :] = out.reshape(HPK // 2, 2 * T, 128).astype(BF)
        stats = [jnp.where(lane < 4 + b, stats[:, 0, i], stats[:, 1, i]) for i, b in enumerate((0, 8))]
        given[0][here, 2 * T :, :] = jnp.where(lane < 8, *stats).astype(BF)


def project_kernel(ids_ref, chances_ref, parts_ref, weight_ref, send_ref, picker_ref, combine_ref):
    prepare(ids_ref, chances_ref, picker_ref, combine_ref)
    stats = parts_ref[:, 2 * T :, :].astype(F32)
    heads = []
    for i in range(2):
        high, low, total, rest = [
            jnp.concatenate([stats[:, :, 8 * b + 4 * i + q : 8 * b + 4 * i + q + 1] for b in range(2)], axis=1)
            for q in range(4)
        ]
        peak = high + low
        total = total + rest
        factor = jnp.exp(peak - jnp.max(peak, axis=0, keepdims=True))
        total = jnp.sum(factor * total, axis=0)
        out = jnp.sum(factor * parts_ref[:, i * T : (i + 1) * T, :].astype(F32), axis=0)
        heads.append((out / total).astype(BF))
    attention = jnp.concatenate(heads, axis=1)
    wide = 512
    for j in range(D // wide):
        block = jnp.dot(attention, weight_ref[:, j * wide : (j + 1) * wide], preferred_element_type=F32).astype(BF)
        for i in range(wide // 128):
            send_ref[j * (wide // 128) + i] = block[:, i * 128 : (i + 1) * 128]


def dispatch_kernel(start_ref, sums_ref, residual_ref, picker_ref, hidden_ref, send_ref):
    here = pl.ds(pl.multiple_of(start_ref[0], 128), 128)
    hidden = residual_ref[:, here].astype(F32) + jnp.sum(sums_ref[...].astype(F32), axis=0)
    hidden_ref[...] = hidden
    send_ref[...] = lax.dot_general(
        picker_ref[...], hidden.astype(BF), (((0,), (0,)), ((), ())), preferred_element_type=F32
    ).astype(BF)


def hidden_units_kernel(rows_ref, gain_ref, gate_ref, up_ref, act_ref, wide_ref, token_ref):
    wide_ref[...] = rows_ref[...].astype(F32)
    for c in range(NC):
        for s in range(CAPE):
            token_ref[s * NG : (s + 1) * NG, c * 128 : (c + 1) * 128] = wide_ref[pl.ds(c * CAPE + s, NG, stride=128), :]
    hidden = token_ref[...]
    normed = (hidden * lax.rsqrt(jnp.mean(hidden * hidden, axis=1, keepdims=True) + EPS) * gain_ref[...]).astype(BF)
    gate = lax.dot_general(normed, gate_ref[...], NT, preferred_element_type=F32)
    up = lax.dot_general(normed, up_ref[...], NT, preferred_element_type=F32)
    act_ref[...] = (gate / (1.0 + jnp.exp(-gate)) * up).astype(BF)


def down_kernel(act_ref, down_ref, send_ref, wide_ref):
    act = act_ref[...]
    wide = 512
    for j in range(D // wide):
        block = jnp.dot(act, down_ref[:, j * wide : (j + 1) * wide], preferred_element_type=F32)
        for i in range(wide // 128):
            for s in range(CAPE):
                wide_ref[pl.ds((j * (wide // 128) + i) * CAPE + s, NG, stride=128), :] = block[
                    s * NG : (s + 1) * NG, i * 128 : (i + 1) * 128
                ]
    send_ref[...] = wide_ref[...].astype(BF)


def combine_kernel(rows_ref, table_ref, hidden_ref, out_ref):
    both = jnp.dot(table_ref[...], rows_ref[...], preferred_element_type=F32)
    out_ref[...] = (hidden_ref[...] + both[:T] + both[T:]).astype(BF)


def shards(
    queries,
    resident_key_cache,
    resident_value_cache,
    res_len,
    visual_page_pool,
    recall_holder,
    recall_slot,
    o_weight,
    residual,
    norm_gain,
    expert_ids,
    expert_weights,
    w_gate,
    w_up,
    w_down,
):
    ctx_index = lax.axis_index(CTX)
    rows = NG * NC * CAPE
    start = (ctx_index * 128).reshape(1).astype(jnp.int32)

    smem = pl.BlockSpec(memory_space=pltpu.SMEM)
    vmem = pl.BlockSpec(memory_space=pltpu.VMEM)
    hbm = pl.BlockSpec(memory_space=pltpu.HBM)
    pages = [visual_page_pool]
    for k in range(1, 4):
        pages.append(lax.ppermute(visual_page_pool, "y", [(i, (i + k) % 4) for i in range(4)]))
    pages += [lax.ppermute(part, "core", [(0, 1), (1, 0)]) for part in pages]

    pad = ((0, 0), (0, 1))
    holder, slot = jnp.pad(recall_holder[0], pad), jnp.pad(recall_slot[0], pad)
    group = holder // NC
    back = (lax.axis_index("y") + 4 - group // 2) % 4
    near = jnp.where(group % 2 == lax.axis_index("core"), back, back + 4)
    key = (holder % NC) * 128 + near * SLOTS + slot
    column = lax.broadcasted_iota(jnp.int32, key.shape, 1)
    key = jnp.where(column < SLOTS, key, res_len[:, None])
    lists, lengths = pl.pallas_call(
        lists_kernel,
        out_shape=(jax.ShapeDtypeStruct((NC, T, 128), BF), jax.ShapeDtypeStruct((T, 128), jnp.int32)),
        compiler_params=params(4),
        cost_estimate=cost(4_000_000, 140_000),
        name="lists",
    )(key)
    lists = lax.all_to_all(lists, CTX, split_axis=0, concat_axis=0, tiled=True)

    wide = jax.ShapeDtypeStruct((HEADS * T, 128), F32)
    out, stats = pl.pallas_call(
        resident_kernel,
        in_specs=[vmem, smem, hbm, hbm, hbm],
        out_shape=(wide, wide),
        scratch_shapes=[
            pltpu.VMEM((HEADS * T, HW), F32),
            pltpu.VMEM((T, HEADS * HW), BF),
            pltpu.VMEM((T, 128, KV * HW), BF),
            pltpu.VMEM((T, 128, KV * HW), BF),
            pltpu.SemaphoreType.DMA((2 * T // FETCH + 1,)),
        ],
        compiler_params=params(51),
        cost_estimate=cost(70_000_000, 6_000_000, 131_072),
        name="resident",
    )(lengths, start, queries, resident_key_cache, resident_value_cache)

    own = pl.pallas_call(
        functools.partial(recalled_kernel, 0),
        out_shape=(wide, wide),
        compiler_params=params(16),
        cost_estimate=cost(270_000_000, 4_000_000, 524_288),
        name="recalled_own",
    )(lists, queries, *pages[:4])
    parts = pl.pallas_call(
        functools.partial(recalled_kernel, 1),
        out_shape=jax.ShapeDtypeStruct((NC, CHUNK, 128), BF),
        compiler_params=params(16),
        cost_estimate=cost(270_000_000, 4_000_000, 524_288),
        name="recalled_other",
    )(lists, queries, *pages[4:], *own, out, stats)
    parts = lax.all_to_all(parts, CTX, split_axis=0, concat_axis=0, tiled=True)

    sums, picker, table = pl.pallas_call(
        project_kernel,
        out_shape=(
            jax.ShapeDtypeStruct((NC, T, 128), BF),
            jax.ShapeDtypeStruct((T, rows), BF),
            jax.ShapeDtypeStruct((2 * T, rows), BF),
        ),
        compiler_params=params(8),
        cost_estimate=cost(44_000_000, 2_900_000, 2048),
        name="project",
    )(expert_ids.T, expert_weights.T, parts, o_weight)
    sums = lax.all_to_all(sums, CTX, split_axis=0, concat_axis=0, tiled=True)

    hidden, send = pl.pallas_call(
        dispatch_kernel,
        in_specs=[smem, vmem, vmem, vmem],
        out_shape=(jax.ShapeDtypeStruct((T, 128), F32), jax.ShapeDtypeStruct((rows, 128), BF)),
        compiler_params=params(8),
        cost_estimate=cost(4_000_000, 500_000),
        name="dispatch",
    )(start, sums, residual, picker)
    arrived = lax.all_to_all(send.reshape(NG * NC, CAPE, 128), ALL, split_axis=0, concat_axis=0, tiled=True)

    act = pl.pallas_call(
        hidden_units_kernel,
        out_shape=jax.ShapeDtypeStruct((NG * CAPE, FP), BF),
        scratch_shapes=[pltpu.VMEM((rows, 128), F32), pltpu.VMEM((NG * CAPE, D), F32)],
        compiler_params=params(8),
        cost_estimate=cost(100_000_000, 3_500_000, 8192),
        name="hidden_units",
    )(arrived.reshape(rows, 128), norm_gain.reshape(1, D), w_gate[0], w_up[0])
    results = pl.pallas_call(
        down_kernel,
        out_shape=jax.ShapeDtypeStruct((rows, 128), BF),
        scratch_shapes=[pltpu.VMEM((rows, 128), F32)],
        compiler_params=params(8),
        cost_estimate=cost(50_000_000, 1_900_000),
        name="down",
    )(act, w_down[0])
    returned = lax.all_to_all(results.reshape(NG * NC, CAPE, 128), ALL, split_axis=0, concat_axis=0, tiled=True)

    return pl.pallas_call(
        combine_kernel,
        out_shape=jax.ShapeDtypeStruct((T, 128), BF),
        compiler_params=params(8),
        cost_estimate=cost(8_000_000, 400_000),
        name="combine",
    )(returned.reshape(rows, 128), table, hidden)


def solution(mesh):
    fine = Mesh(mesh.devices.reshape(4, 2, 4, 8), ALL)
    placed = (
        P(GRP, None),
        P(GRP, CTX, None),
        P(GRP, CTX, None),
        P(GRP),
        P(ALL, None, None, None),
        P(CTX, GRP, None),
        P(CTX, GRP, None),
        P(CTX, None),
        P(GRP, None),
        P(),
        P(GRP, None),
        P(GRP, None),
        P(ALL, None, None),
        P(ALL, None, None),
        P(ALL, None, None),
    )
    return jax.shard_map(shards, mesh=fine, in_specs=placed, out_specs=P(GRP, CTX), check_vma=False)
```
